128 devices in a mesh: sec: 4 (over x_hi, core), region: 32 (over y, x_lo, z).
Axes of the slice: x: 4 (x_hi: 2, x_lo: 2; x = x_hi * 2 + x_lo), y: 4, z: 4, core: 2. Of those that a mesh axis runs over, the one named last changes fastest.
Arguments:
- windows: bfloat16 [4, 1536, 25600], P('sec', 'region'), may hold values from -24 to 24
- partner_dev: int32 [1536], P('region'), may hold values from 0 to 31, as said below
- partner_slot: int32 [1536], P('region'), may hold values from 0 to 47
Outputs:
- montage_flow: float32 [4, 2, 1536], P('sec', None, 'region')
- section_flow: float32 [4, 2, 1536], P('sec', None, 'region')
- displacement: float32 [4, 2, 1536], P('sec', None, 'region')
The draws below stay inside these ranges and needn't reach their ends.
Inputs may be any that keep to these rules, and one draw needn't show every extreme that they name: The pairing is symmetric: the partner of window j is window partner_dev[j] * 48 + partner_slot[j], and that window's partner is j; the same pairing holds in every section. No window's partner lies on its own device, and for every two devices either none or exactly 3 of one device's windows have partners on the other.
All inputs are finite; a program needn't handle non-finite values.
Results may differ from the reference program's by a relative error of at most 0.00038.
Values may be sent and summed in bfloat16 or wider, within the bound.
A program may use at most 128 MiB of HBM per device.

```python
import math
import jax
import jax.numpy as jnp
from jax import lax

WIN = 160
RADIUS = 16
SHIFTS = 33
WIN_DEV = 48
CAP = 3
ITERS = 32
SECTIONS = 4
WINDOWS = 1536
N_REGION = 32


def pairing(key):
    regions = WINDOWS // WIN_DEV
    groups = WIN_DEV // (2 * CAP)
    key_label, key_offset, key_slots = jax.random.split(key, 3)
    labels = jax.random.permutation(key_label, regions)
    owners = jnp.argsort(labels, stable=True)
    offsets = jax.random.permutation(key_offset, regions // 2 - 1)[:groups] + 1
    codes = jax.vmap(lambda sub_key: jax.random.permutation(sub_key, WIN_DEV))(jax.random.split(key_slots, regions))
    slots_of = jnp.argsort(codes, axis=1, stable=True)
    group_ids = codes // CAP
    places = codes % CAP
    step_sizes = jnp.where(group_ids < groups, offsets[group_ids % groups], -offsets[group_ids % groups])
    partner_devices = owners[(labels[:, None] + step_sizes) % regions]
    partner_codes = (group_ids + groups) % (2 * groups) * CAP + places
    partner_slots = slots_of[partner_devices, partner_codes]
    return (partner_devices.reshape(-1).astype(jnp.int32), partner_slots.reshape(-1).astype(jnp.int32))


def draw_partner_dev(key, part):
    return pairing(key)[0]


def draw_partner_slot(key, part):
    return pairing(key)[1]


def draw_windows(key, part):
    devices, slots = pairing(key)
    key = jax.random.fold_in(key, 7)
    key_base, key_shift, key_noise = jax.random.split(key, 3)
    whole = jnp.arange(WINDOWS, dtype=jnp.int32)
    pair_ids = jnp.minimum(whole, devices * WIN_DEV + slots)
    base = jnp.clip(jax.random.normal(key_base, (WINDOWS, WIN, WIN), jnp.float32), -4.0, 4.0)
    moves = jax.random.randint(key_shift, (SECTIONS, WINDOWS, 2), -(RADIUS // 2), RADIUS // 2 + 1)
    pixel_axis = jnp.arange(WIN, dtype=jnp.int32)
    rows = (pixel_axis[None, None, :] - moves[:, :, 0:1]) % WIN
    cols = (pixel_axis[None, None, :] - moves[:, :, 1:2]) % WIN
    moved = base[pair_ids[None, :, None, None], rows[:, :, :, None], cols[:, :, None, :]]
    shape = (SECTIONS, WINDOWS, WIN, WIN)
    noise = 0.7 * jnp.clip(jax.random.normal(key_noise, shape, jnp.float32), -3.0, 3.0)
    return (moved + noise).reshape(SECTIONS, WINDOWS, WIN * WIN).astype(jnp.bfloat16)


def setup_inputs(seed: int = 0) -> dict:
    key_list = jax.random.split(jax.random.key(seed), 4)
    return {
        "windows": draw_windows(jax.random.fold_in(key_list[3], 71), 0),
        "partner_dev": draw_partner_dev(jax.random.fold_in(key_list[3], 71), 0),
        "partner_slot": draw_partner_slot(jax.random.fold_in(key_list[3], 71), 0),
    }


sharpness = 12.0
montage_stiffness = 1.0
section_stiffness = 1.0
anchor_stiffness = 0.05
step_length = 0.2

def dft_tables():
    indices = jnp.arange(WIN, dtype=jnp.int32)
    phase_index = indices[:, None] * indices[None, :] % WIN
    angles = phase_index.astype(jnp.float32) * (2.0 * math.pi / WIN)
    cosine_table = jnp.cos(angles).astype(jnp.bfloat16)
    sine_table = jnp.sin(angles).astype(jnp.bfloat16)
    offsets = jnp.arange(SHIFTS, dtype=jnp.int32) - RADIUS
    back_phase = offsets[:, None] * indices[None, :] % WIN
    back_angles = back_phase.astype(jnp.float32) * (2.0 * math.pi / WIN)
    back_cos = jnp.cos(back_angles).astype(jnp.bfloat16)
    back_sin = jnp.sin(back_angles).astype(jnp.bfloat16)
    return (cosine_table, sine_table, back_cos, back_sin, offsets)

def spectra_block(images, cosine_table, sine_table):
    window_count = images.shape[0]
    square = images.reshape(window_count, WIN, WIN).astype(jnp.float32)
    right_table = jnp.concatenate([cosine_table, -sine_table], axis=1).astype(jnp.float32)
    first_segment = jnp.einsum('bxy,yk->bxk', square, right_table).astype(jnp.bfloat16)
    left_table = jnp.concatenate([cosine_table, sine_table], axis=0).astype(jnp.float32)
    products = jnp.einsum('kx,bxj->bkj', left_table, first_segment.astype(jnp.float32))
    spec_real = products[:, :WIN, :WIN] + products[:, WIN:, WIN:]
    spec_imag = products[:, :WIN, WIN:] - products[:, WIN:, :WIN]
    return jnp.concatenate([spec_real, spec_imag], axis=2).astype(jnp.bfloat16)

def spectral_energy(spectrum):
    values = spectrum.astype(jnp.float32)
    return lax.optimization_barrier(jnp.sum(values * values, axis=(1, 2))) / (WIN * WIN)

def correlate_block(first_spec, second_spec, first_energy, second_energy, back_cos, back_sin, offsets):
    first_real = first_spec[:, :, :WIN].astype(jnp.float32)
    first_imag = first_spec[:, :, WIN:].astype(jnp.float32)
    second_real = second_spec[:, :, :WIN].astype(jnp.float32)
    second_imag = second_spec[:, :, WIN:].astype(jnp.float32)
    cross_real = (first_real * second_real + first_imag * second_imag) / (WIN * WIN)
    cross_imag = (first_imag * second_real - first_real * second_imag) / (WIN * WIN)
    cross_power = jnp.concatenate([cross_real, cross_imag], axis=2).astype(jnp.bfloat16)
    back_left = jnp.concatenate([back_cos, back_sin], axis=0).astype(jnp.float32)
    partial_back = jnp.einsum('sk,bkj->bsj', back_left, cross_power.astype(jnp.float32))
    back_real = partial_back[:, :SHIFTS, :WIN] - partial_back[:, SHIFTS:, WIN:]
    back_imag = partial_back[:, :SHIFTS, WIN:] + partial_back[:, SHIFTS:, :WIN]
    half_back = jnp.concatenate([back_real, back_imag], axis=2).astype(jnp.bfloat16)
    back_right = jnp.concatenate([back_cos.T, -back_sin.T], axis=0).astype(jnp.float32)
    surface = jnp.einsum('bsj,jt->bst', half_back.astype(jnp.float32), back_right)
    normed = surface / jnp.sqrt(first_energy * second_energy + 1e-06)[:, None, None]
    weights = jnp.exp(sharpness * normed)
    weight_total = lax.optimization_barrier(jnp.sum(weights, axis=(1, 2)))
    shift_values = offsets.astype(jnp.float32)
    row_flow = lax.optimization_barrier(jnp.sum(weights * shift_values[None, :, None], axis=(1, 2))) / weight_total
    col_flow = lax.optimization_barrier(jnp.sum(weights * shift_values[None, None, :], axis=(1, 2))) / weight_total
    return jnp.stack([row_flow, col_flow], axis=1)

def reference(windows, partner_dev, partner_slot):
    cosine_table, sine_table, back_cos, back_sin, offsets = dft_tables()
    grouped = windows.reshape(SECTIONS * N_REGION, WIN_DEV, WIN * WIN)
    spectra = lax.map(lambda images: spectra_block(images, cosine_table, sine_table), grouped)
    spectra = spectra.reshape(SECTIONS, WINDOWS, WIN, 2 * WIN)
    energies = lax.map(spectral_energy, spectra)
    partner_index = (partner_dev * WIN_DEV + partner_slot).astype(jnp.int32)

    def pair_flows(first_spec, second_spec, first_energy, second_energy):
        members = (first_spec.reshape(N_REGION, WIN_DEV, WIN, 2 * WIN), second_spec.reshape(N_REGION, WIN_DEV, WIN, 2 * WIN), first_energy.reshape(N_REGION, WIN_DEV), second_energy.reshape(N_REGION, WIN_DEV))
        flows = lax.map(lambda parts: correlate_block(parts[0], parts[1], parts[2], parts[3], back_cos, back_sin, offsets), members)
        return flows.reshape(WINDOWS, 2)

    def section_flows(sec_index):
        following_index = jnp.minimum(sec_index + 1, SECTIONS - 1).astype(jnp.int32)
        current = spectra[sec_index]
        current_energy = energies[sec_index]
        following = spectra[following_index]
        following_energy = energies[following_index]
        montage = pair_flows(current, current[partner_index], current_energy, current_energy[partner_index])
        section = pair_flows(current, following, current_energy, following_energy)
        section = jnp.where(sec_index < SECTIONS - 1, section, 0.0)
        return (montage, section)
    montage, section = lax.map(section_flows, jnp.arange(SECTIONS, dtype=jnp.int32))
    disagreement = montage - montage[:, partner_index]
    zero_layer = jnp.zeros((1, WINDOWS, 2), jnp.float32)
    previous_flow = jnp.concatenate([zero_layer, section[:-1]], axis=0)
    sec_ids = jnp.arange(SECTIONS, dtype=jnp.int32)
    has_next = jnp.where(sec_ids < SECTIONS - 1, 1.0, 0.0).astype(jnp.float32)[:, None, None]
    has_prev = jnp.where(sec_ids > 0, 1.0, 0.0).astype(jnp.float32)[:, None, None]

    def relax(turn_index, shift_field):
        partner_field = shift_field[:, partner_index]
        next_field = jnp.concatenate([shift_field[1:], zero_layer], axis=0)
        previous_field = jnp.concatenate([zero_layer, shift_field[:-1]], axis=0)
        gradient = montage_stiffness * (2.0 * shift_field - 2.0 * partner_field - disagreement) + section_stiffness * has_next * (shift_field - next_field - section) - section_stiffness * has_prev * (previous_field - shift_field - previous_flow) + anchor_stiffness * shift_field
        return shift_field - step_length * gradient
    shift_field = lax.fori_loop(0, ITERS, relax, jnp.zeros((SECTIONS, WINDOWS, 2), jnp.float32))
    return (jnp.transpose(montage, (0, 2, 1)), jnp.transpose(section, (0, 2, 1)), jnp.transpose(shift_field, (0, 2, 1)))
```

```python
import functools
import math

import jax
import jax.numpy as jnp
import ml_dtypes
import numpy as np
from jax import lax
from jax.experimental import pallas as pl
from jax.experimental.pallas import tpu as pltpu
from jax.sharding import PartitionSpec as P

WIN = 160
RADIUS = 16
SHIFTS = 33
ITERS = 32
HALF = WIN // 2 + 1
CAP = 3
REGIONS = 32
SECTIONS = 4
WIN_DEV = 48
GROUPS = WIN_DEV // CAP
SHARE = 12
CHUNK = 4
QROWS = 48
TLANES = 40
PHASES = 4
QUARTER = WIN // PHASES

sharpness = 12.0
montage_stiffness = 1.0
section_stiffness = 1.0
anchor_stiffness = 0.05
step_length = 0.2

F32 = jnp.float32
BF16 = jnp.bfloat16
MESH = pl.DeviceIdType.MESH
EMPTY = (1 << 20) + 63


def tables():
    f32 = np.float32
    index = np.arange(WIN)
    step = f32(2.0 * math.pi / WIN)

    def rounded(fn, phase):
        angle = (phase % WIN).astype(f32) * step
        return fn(angle.astype(np.float64)).astype(f32).astype(ml_dtypes.bfloat16).astype(f32)

    phase = index[:, None] * index[None, :]
    cosine, sine = rounded(np.cos, phase), rounded(np.sin, phase)
    back = (np.arange(SHIFTS) - RADIUS)[:, None] * index[None, :]
    back_cos, back_sin = rounded(np.cos, back), rounded(np.sin, back)

    right = np.zeros((PHASES, 256, 256), f32)
    for m in range(PHASES):
        rows = slice(32 * m, 32 * m + WIN)
        right[m, rows, :HALF] = cosine[:, :HALF]
        right[m, rows, 128 : 128 + HALF] = -sine[:, :HALF]
    order = np.concatenate([np.arange(QUARTER) * PHASES + m for m in range(PHASES)])
    c, s = cosine[:, order], sine[:, order]
    left = np.concatenate([np.concatenate([c, s], 1), np.concatenate([-s, c], 1)], 0)
    back_left = np.zeros((2 * QROWS, 2 * WIN), f32)
    back_left[:SHIFTS] = np.concatenate([back_cos, -back_sin], 1)
    back_left[QROWS : QROWS + SHIFTS] = np.concatenate([back_sin, back_cos], 1)
    weight = np.full(HALF, 2.0, f32)
    weight[0] = weight[-1] = 1.0
    back_right = np.zeros((512, 128), f32)
    energy = np.zeros((256, 128), f32)
    member = np.zeros((2, 8, 128), f32)
    for i in range(CAP):
        rows, lanes = HALF * i, TLANES * i
        back_right[rows : rows + HALF, lanes : lanes + SHIFTS] = weight[:, None] * back_cos[:, :HALF].T
        back_right[256 + rows : 256 + rows + HALF, lanes : lanes + SHIFTS] = (
            -weight[:, None] * back_sin[:, :HALF].T
        )
        energy[rows : rows + HALF, lanes : lanes + TLANES] = weight[:, None]
        member[0, i, lanes : lanes + SHIFTS] = 1.0
        member[1, CAP + i, lanes : lanes + SHIFTS] = 1.0
    return [jnp.asarray(t.astype(ml_dtypes.bfloat16)) for t in (right, left, back_left, back_right, energy, member)]


def split3(x):
    high = x.astype(BF16)
    rest = x - high.astype(F32)
    middle = rest.astype(BF16)
    low = (rest - middle.astype(F32)).astype(BF16)
    return high, middle, low


def exact_dot(x, table):
    rows = x.shape[0]
    out = jnp.dot(jnp.concatenate(split3(x), axis=0), table, preferred_element_type=F32)
    return out[:rows] + out[rows : 2 * rows] + out[2 * rows :]


def lane_iota(rows=1):
    return lax.broadcasted_iota(jnp.int32, (rows, 128), 1)


def spectra_kernel(
    win_ref, dev_ref, slot_ref, right_ref, left_ref,
    group_ref, slots_ref, place_ref, pick_ref,
    seg_re, seg_im, out_buf, codes, offsets, group_sem, slot_sem,
):
    me = lax.axis_index("region")
    sec = lax.axis_index("sec")

    def clear(k, _):
        codes[k] = EMPTY
        return 0

    lax.fori_loop(0, CAP * REGIONS, clear, 0)

    def insert(j, _):
        device = dev_ref[j]
        offset = (device - me + REGIONS) % REGIONS
        own = jnp.logical_or(
            offset < REGIONS // 2, jnp.logical_and(offset == REGIONS // 2, me < device)
        )
        new = jnp.where(own, j, slot_ref[j]) * 64 + j
        at = CAP * offset
        a, b, c = codes[at], codes[at + 1], codes[at + 2]
        codes[at] = jnp.minimum(a, new)
        new = jnp.maximum(a, new)
        codes[at + 1] = jnp.minimum(b, new)
        new = jnp.maximum(b, new)
        codes[at + 2] = jnp.minimum(c, new)
        return 0

    lax.fori_loop(0, WIN_DEV, insert, 0)

    def compact(o, count):
        offsets[count] = o
        return count + jnp.where(codes[CAP * o] < EMPTY, 1, 0)

    lax.fori_loop(1, REGIONS, compact, 0)

    for m in range(PHASES):
        for part in range(5):
            rows = [
                win_ref[:, 640 * q + 128 * m : 640 * q + 128 * m + 256]
                for q in range(8 * part, 8 * part + 8)
            ]
            seg = jnp.dot(
                jnp.concatenate(rows, axis=0), right_ref[m], preferred_element_type=F32
            )
            start = (QUARTER * m + 8 * part) * WIN_DEV
            seg_re[start : start + 8 * WIN_DEV, :] = seg[:, :128]
            seg_im[start : start + 8 * WIN_DEV, :] = seg[:, 128:]

    place_ref[...] = jnp.zeros_like(place_ref)
    lane = lane_iota()
    wide = lane_iota(WIN)

    def group(g, picks):
        o = offsets[g]
        members = [codes[CAP * o + i] % 64 for i in range(CAP)]
        sides = []
        for seg in (seg_re, seg_im):
            x0, x1, x2 = [seg[pl.ds(w, WIN, stride=WIN_DEV), :] for w in members]
            x1 = pltpu.roll(x1, HALF, 1)
            x2 = pltpu.roll(x2, 2 * HALF - 128, 1)
            sides.append(
                jnp.concatenate(
                    [jnp.where(wide < HALF, x0, x1), jnp.where(wide < 2 * HALF - 128, x1, x2)],
                    axis=1,
                ).astype(BF16)
            )
        spectrum = jnp.dot(
            left_ref[...], jnp.concatenate(sides, axis=0), preferred_element_type=F32
        )
        out_buf[g] = spectrum.astype(BF16)
        pltpu.make_async_copy(out_buf.at[g], group_ref.at[g], group_sem.at[g]).start()
        pltpu.make_async_copy(out_buf.at[g], slots_ref.at[o], slot_sem.at[g]).start()
        for edge in range(SECTIONS - 1):
            row = (lane == REGIONS * edge + o).astype(F32)
            place_ref[pl.ds(GROUPS * edge + g, 1), :] = row
        valid = jnp.where(lane % REGIONS == o, 1, picks[CAP])
        return tuple(
            jnp.where(lane == w, REGIONS * sec + o, pick) for w, pick in zip(members, picks)
        ) + (valid,)

    start = tuple(jnp.full((1, 128), -1, jnp.int32) for _ in range(CAP))
    picks = lax.fori_loop(0, GROUPS, group, start + (jnp.zeros((1, 128), jnp.int32),))
    pick_ref[...] = jnp.concatenate(picks + picks, axis=0)

    def finish(g, _):
        o = offsets[g]
        pltpu.make_async_copy(out_buf.at[g], group_ref.at[g], group_sem.at[g]).wait()
        pltpu.make_async_copy(out_buf.at[g], slots_ref.at[o], slot_sem.at[g]).wait()
        return 0

    lax.fori_loop(0, GROUPS, finish, 0)


SECTION_RECV = (
    ((1, 0), (1, 1), (1, 2)),
    ((0, 3), (2, 0), (2, 1)),
    ((1, 2), (1, 3), (3, 0)),
    ((2, 1), (2, 2), (2, 3)),
)


def section_sends(section):
    return [
        (to, source, chunk)
        for to in range(SECTIONS)
        for chunk, (origin, source) in enumerate(SECTION_RECV[to])
        if origin == section
    ]


def flow_kernel(
    group_ref, slots_ref, place_ref, back_left_ref, back_right_ref, energy_ref, member_ref,
    out_ref,
    local_groups, local_slots, from_section, from_region, cross, backs, squares, sums, gathered, mine, field, fields,
    local_sem, sec_send, sec_recv, reg_send, reg_recv, p1_send, p1_recv, p2_send, p2_recv,
):
    me = lax.axis_index("region")
    sec = lax.axis_index("sec")
    half = REGIONS // 2

    def neighbour(o):
        return {"region": (me + o) % REGIONS}

    barrier = pltpu.get_barrier_semaphore()

    def greet(o, _):
        pl.semaphore_signal(barrier, inc=1, device_id=neighbour(o), device_id_type=MESH)
        return 0

    lax.fori_loop(1, REGIONS, greet, 0)
    for d in range(1, SECTIONS):
        pl.semaphore_signal(
            barrier, inc=1, device_id={"sec": (sec + d) % SECTIONS}, device_id_type=MESH
        )
    pl.semaphore_wait(barrier, REGIONS - 1 + SECTIONS - 1)

    def section_copy(k, index):
        to, source, chunk = section_sends(k)[index]
        return pltpu.make_async_remote_copy(
            src_ref=group_ref.at[pl.ds(CHUNK * source, CHUNK)],
            dst_ref=from_section.at[pl.ds(CHUNK * chunk, CHUNK)],
            send_sem=sec_send.at[index],
            recv_sem=sec_recv.at[chunk],
            device_id={"sec": to},
            device_id_type=MESH,
        )

    def region_copy(o):
        return pltpu.make_async_remote_copy(
            src_ref=slots_ref.at[o],
            dst_ref=from_region.at[o - 1],
            send_sem=reg_send.at[o - 1],
            recv_sem=reg_recv.at[o - 1],
            device_id=neighbour(o),
            device_id_type=MESH,
        )

    for k in range(SECTIONS):

        @pl.when(sec == k)
        def _():
            for index in range(len(section_sends(k))):
                section_copy(k, index).start()

    def send_region(o, _):
        region_copy(o).start()
        return 0

    lax.fori_loop(1, half + 1, send_region, 0)

    keep_slots = pltpu.make_async_copy(slots_ref.at[pl.ds(half, half)], local_slots, local_sem.at[0])
    keep_groups = pltpu.make_async_copy(group_ref, local_groups, local_sem.at[1])
    keep_slots.start()
    keep_groups.start()
    sums[...] = jnp.zeros_like(sums)
    keep_slots.wait()
    keep_groups.wait()

    lane = lane_iota()
    row_shift = lax.broadcasted_iota(jnp.int32, (QROWS, 128), 0)
    shift_mask = jnp.logical_and(row_shift < SHIFTS, lane_iota(QROWS) % TLANES < SHIFTS)
    row_value = (row_shift - RADIUS).astype(F32)

    def correlate(first_ref, second_ref, u):
        energy_a = jnp.zeros((8, 256), F32)
        energy_b = jnp.zeros((8, 256), F32)
        for r in range(0, WIN, 32):
            ar = first_ref[r : r + 32, :].astype(F32)
            ai = first_ref[WIN + r : WIN + r + 32, :].astype(F32)
            br = second_ref[r : r + 32, :].astype(F32)
            bi = second_ref[WIN + r : WIN + r + 32, :].astype(F32)
            scale = 1.0 / (WIN * WIN)
            cross[u, r : r + 32, :] = ((ar * br + ai * bi) * scale).astype(BF16)
            cross[u, WIN + r : WIN + r + 32, :] = ((ai * br - ar * bi) * scale).astype(BF16)
            energy_a += jnp.sum((ar * ar + ai * ai).reshape(4, 8, 256), axis=0)
            energy_b += jnp.sum((br * br + bi * bi).reshape(4, 8, 256), axis=0)
        squares[16 * u : 16 * u + 8, :] = energy_a
        squares[16 * u + 8 : 16 * u + 16, :] = energy_b
        back = jnp.dot(back_left_ref[...], cross[u], preferred_element_type=F32).astype(BF16)
        backs[QROWS * u : QROWS * u + QROWS, :256] = back[:QROWS]
        backs[QROWS * u : QROWS * u + QROWS, 256:] = back[QROWS:]

    def weigh(rows):
        surfaces = jnp.dot(backs[...], back_right_ref[...], preferred_element_type=F32)
        energies = exact_dot(squares[...], energy_ref[...]) / (WIN * WIN)
        for u, row in enumerate(rows):
            first = jnp.sum(energies[16 * u : 16 * u + 8], axis=0, keepdims=True)
            second = jnp.sum(energies[16 * u + 8 : 16 * u + 16], axis=0, keepdims=True)
            norm = jnp.sqrt(first * second + 1e-06)
            surface = surfaces[QROWS * u : QROWS * u + QROWS]
            weights = jnp.where(shift_mask, jnp.exp(sharpness * (surface / norm)), 0.0)
            sums[0, pl.ds(row, 1), :] = jnp.sum(weights, axis=0, keepdims=True)
            sums[1, pl.ds(row, 1), :] = jnp.sum(weights * row_value, axis=0, keepdims=True)

    def section_batch(chunk, _):
        pltpu.make_async_remote_copy(
            src_ref=group_ref.at[pl.ds(0, CHUNK)],
            dst_ref=from_section.at[pl.ds(CHUNK * chunk, CHUNK)],
            send_sem=sec_send.at[0],
            recv_sem=sec_recv.at[chunk],
            device_id={"sec": (sec + 1) % SECTIONS},
            device_id_type=MESH,
        ).wait_recv()
        start = CHUNK * ((SHARE // CHUNK * sec + chunk) % CHUNK)
        for u in range(CHUNK):
            correlate(local_groups.at[start + u], from_section.at[CHUNK * chunk + u], u)
        weigh([half + CHUNK * chunk + u for u in range(CHUNK)])
        return 0

    lax.fori_loop(0, SHARE // CHUNK, section_batch, 0)

    def region_batch(batch, _):
        for u in range(CHUNK):
            o = CHUNK * batch + u + 1
            region_copy(o).wait_recv()
            correlate(local_slots.at[half - o], from_region.at[o - 1], u)
        weigh([half - (CHUNK * batch + u + 1) for u in range(CHUNK)])
        return 0

    lax.fori_loop(0, half // CHUNK, region_batch, 0)

    nt = (((1,), (1,)), ((), ()))

    def turned(table, x):
        parts = [
            lax.dot_general(table, part, nt, preferred_element_type=F32) for part in split3(x)
        ]
        return parts[0] + parts[1] + parts[2]

    column_value = (lane % TLANES - RADIUS).astype(F32)
    total = turned(member_ref[0] + member_ref[1], sums[0])
    moment = turned(member_ref[0], sums[1]) + turned(member_ref[1], sums[0] * column_value)
    flows = moment / jnp.where(total == 0.0, 1.0, total)
    lane8 = lane_iota(8)
    swapped = jnp.logical_and(lane8 >= half, lane8 < half + CHUNK * sec)
    flows = jnp.where(swapped, -flows, flows)
    mine[...] = flows

    def p1_copy(d):
        return pltpu.make_async_remote_copy(
            src_ref=mine,
            dst_ref=gathered.at[d - 1],
            send_sem=p1_send.at[d - 1],
            recv_sem=p1_recv.at[d - 1],
            device_id={"sec": (sec + d) % SECTIONS},
            device_id_type=MESH,
        )

    for d in range(1, SECTIONS):
        p1_copy(d).start()
    for d in range(1, SECTIONS):
        p1_copy(d).wait_recv()
    montage = jnp.zeros((8, 128), F32)
    section = jnp.zeros((8, 128), F32)
    for k in range(SECTIONS):
        block = flows
        for d in range(1, SECTIONS):
            block = jnp.where((sec - k + SECTIONS) % SECTIONS == d, gathered[d - 1], block)
        moved = pltpu.roll(block, (REGIONS * k + half) % 128, 1)
        here = jnp.logical_and(lane8 >= REGIONS * k + half, lane8 < REGIONS * k + REGIONS)
        montage = jnp.where(here, moved, montage)
        moved = pltpu.roll(block, (SHARE * k - half + 128) % 128, 1)
        here = jnp.logical_and(lane8 >= SHARE * k, lane8 < SHARE * k + SHARE)
        section = jnp.where(here, moved, section)
    section = exact_dot(section, place_ref[...].astype(BF16))
    field[0] = montage
    field[1] = section
    fields[0] = field[...]

    def p2_copy(o):
        return pltpu.make_async_remote_copy(
            src_ref=field,
            dst_ref=fields.at[REGIONS - o],
            send_sem=p2_send.at[o - 1],
            recv_sem=p2_recv.at[REGIONS - 1 - o],
            device_id=neighbour(o),
            device_id_type=MESH,
        )

    def p2_start(o, _):
        p2_copy(o).start()
        return 0

    def p2_wait(o, _):
        p2_copy(o).wait_recv()
        return 0

    lax.fori_loop(1, REGIONS, p2_start, 0)
    lax.fori_loop(1, REGIONS, p2_wait, 0)
    out_ref[...] = fields[...]

    for k in range(SECTIONS):

        @pl.when(sec == k)
        def _():
            for index in range(len(section_sends(k))):
                section_copy(k, index).wait_send()

    def sent_region(o, _):
        region_copy(o).wait_send()
        return 0

    lax.fori_loop(1, half + 1, sent_region, 0)
    for d in range(1, SECTIONS):
        p1_copy(d).wait_send()

    def p2_sent(o, _):
        p2_copy(o).wait_send()
        return 0

    lax.fori_loop(1, REGIONS, p2_sent, 0)


def relax_kernel(fields_ref, pick_ref, montage_ref, section_ref, shift_ref):
    lane8 = lane_iota(8)
    slot = lane8 % REGIONS
    valid = jnp.broadcast_to(pick_ref[CAP : CAP + 1, :], (8, 128)) == 1
    montage = fields_ref[0, 0]
    section = fields_ref[0, 1]
    partner_section = jnp.zeros((8, 128), F32)
    for o in range(1, REGIONS):
        turn = (2 * o - REGIONS) % 128
        here = slot == o
        theirs = fields_ref[o, 1]
        partner_section = jnp.where(here, pltpu.roll(theirs, turn, 1) if turn else theirs, partner_section)
        if o < REGIONS // 2:
            montage = jnp.where(here, -pltpu.roll(fields_ref[o, 0], turn, 1), montage)
    montage = jnp.where(valid, montage, 0.0)
    section = jnp.where(valid, section, 0.0)
    partner_section = jnp.where(valid, partner_section, 0.0)
    has_next = jnp.where(lane8 < REGIONS * (SECTIONS - 1), 1.0, 0.0)
    has_prev = jnp.where(lane8 >= REGIONS, 1.0, 0.0)
    disagreement = 2.0 * montage

    def before(x):
        return pltpu.roll(x, REGIONS, 1)

    def after(x):
        return pltpu.roll(x, 128 - REGIONS, 1)

    def step(u, p, apart, flow, previous):
        gradient = (
            montage_stiffness * (2.0 * u - 2.0 * p - apart)
            + section_stiffness * has_next * (u - after(u) - flow)
            - section_stiffness * has_prev * (before(u) - u - previous)
            + anchor_stiffness * u
        )
        return u - step_length * gradient

    previous, partner_previous = before(section), before(partner_section)

    def turn(_, state):
        u, p = state
        return (
            step(u, p, disagreement, section, previous),
            step(p, u, -disagreement, partner_section, partner_previous),
        )

    zero = jnp.zeros((8, 128), F32)
    shift, _ = lax.fori_loop(0, ITERS, turn, (zero, zero))

    values = jnp.concatenate([montage, section, shift], axis=0)
    row = lax.broadcasted_iota(jnp.int32, (128, 128), 0)
    picked = []
    for i in range(CAP):
        wanted = jnp.broadcast_to(pick_ref[i : i + 1, :], (128, 128))
        picked.append(exact_dot(values, (row == wanted).astype(F32).astype(BF16)))
    for k, ref in enumerate((montage_ref, section_ref, shift_ref)):
        for c in range(2):
            total = sum(picked[i][8 * k + CAP * c + i : 8 * k + CAP * c + i + 1] for i in range(CAP))
            ref[0, c : c + 1, :] = total[:, :WIN_DEV]


VMEM = pl.BlockSpec(memory_space=pltpu.VMEM)
SMEM = pl.BlockSpec(memory_space=pltpu.SMEM)
ANY = pl.BlockSpec(memory_space=pl.ANY)


def body(windows, partner_dev, partner_slot):
    right, left, back_left, back_right, energy, member = tables()
    side = (2 * WIN, 256)
    groups, slots, place, pick = pl.pallas_call(
        spectra_kernel,
        out_shape=(
            jax.ShapeDtypeStruct((GROUPS,) + side, BF16),
            jax.ShapeDtypeStruct((REGIONS,) + side, BF16),
            jax.ShapeDtypeStruct((128, 128), F32),
            jax.ShapeDtypeStruct((8, 128), jnp.int32),
        ),
        in_specs=[VMEM, SMEM, SMEM, VMEM, VMEM],
        out_specs=(ANY, ANY, VMEM, VMEM),
        scratch_shapes=[
            pltpu.VMEM((WIN * WIN_DEV, 128), F32),
            pltpu.VMEM((WIN * WIN_DEV, 128), F32),
            pltpu.VMEM((GROUPS,) + side, BF16),
            pltpu.SMEM((CAP * REGIONS,), jnp.int32),
            pltpu.SMEM((REGIONS,), jnp.int32),
            pltpu.SemaphoreType.DMA((GROUPS,)),
            pltpu.SemaphoreType.DMA((GROUPS,)),
        ],
        compiler_params=pltpu.CompilerParams(vmem_limit_bytes=48 << 20),
        name="spectra",
    )(windows[0], partner_dev, partner_slot, right, left)
    half = REGIONS // 2
    fields = pl.pallas_call(
        flow_kernel,
        out_shape=jax.ShapeDtypeStruct((REGIONS, 2, 8, 128), F32),
        in_specs=[ANY, ANY, VMEM, VMEM, VMEM, VMEM, VMEM],
        out_specs=VMEM,
        scratch_shapes=[
            pltpu.VMEM((GROUPS,) + side, BF16),
            pltpu.VMEM((half,) + side, BF16),
            pltpu.VMEM((SHARE,) + side, BF16),
            pltpu.VMEM((half,) + side, BF16),
            pltpu.VMEM((CHUNK,) + side, BF16),
            pltpu.VMEM((CHUNK * QROWS, 512), BF16),
            pltpu.VMEM((CHUNK * 16, 256), F32),
            pltpu.VMEM((2, 128, 128), F32),
            pltpu.VMEM((SECTIONS - 1, 8, 128), F32),
            pltpu.VMEM((8, 128), F32),
            pltpu.VMEM((2, 8, 128), F32),
            pltpu.VMEM((REGIONS, 2, 8, 128), F32),
            pltpu.SemaphoreType.DMA((2,)),
            pltpu.SemaphoreType.DMA((5,)),
            pltpu.SemaphoreType.DMA((SHARE // CHUNK,)),
            pltpu.SemaphoreType.DMA((half,)),
            pltpu.SemaphoreType.DMA((half,)),
            pltpu.SemaphoreType.DMA((SECTIONS - 1,)),
            pltpu.SemaphoreType.DMA((SECTIONS - 1,)),
            pltpu.SemaphoreType.DMA((REGIONS - 1,)),
            pltpu.SemaphoreType.DMA((REGIONS - 1,)),
        ],
        compiler_params=pltpu.CompilerParams(
            vmem_limit_bytes=48 << 20, collective_id=0, has_side_effects=True
        ),
        name="flows",
    )(groups, slots, place, back_left, back_right, energy, member)
    out = jax.ShapeDtypeStruct((1, 2, WIN_DEV), F32)
    return pl.pallas_call(
        relax_kernel,
        out_shape=(out, out, out),
        in_specs=[VMEM, VMEM],
        out_specs=(VMEM, VMEM, VMEM),
        name="relax",
    )(fields, pick)


def solution(mesh):
    placed = (P("sec", "region", None), P("region"), P("region"))
    return jax.shard_map(
        body,
        mesh=mesh,
        in_specs=placed,
        out_specs=(P("sec", None, "region"),) * 3,
        check_vma=False,
    )
```

```python
import functools
import math

import jax
import jax.numpy as jnp
import ml_dtypes
import numpy as np
from jax import lax
from jax.experimental import pallas as pl
from jax.experimental.pallas import tpu as pltpu
from jax.sharding import PartitionSpec as P

WIN = 160
RADIUS = 16
SHIFTS = 33
ITERS = 32
HALF = WIN // 2 + 1
CAP = 3
REGIONS = 32
SECTIONS = 4
WIN_DEV = 48
GROUPS = WIN_DEV // CAP
SHARE = 12
CHUNK = 4
QROWS = 48
TLANES = 40
PHASES = 4
QUARTER = WIN // PHASES
PARTS = 5
STEPS_DEV = REGIONS // 2
QUARTERS = GROUPS // CHUNK

sharpness = 12.0
montage_stiffness = 1.0
section_stiffness = 1.0
anchor_stiffness = 0.05
step_length = 0.2

F32 = jnp.float32
BF16 = jnp.bfloat16
MESH = pl.DeviceIdType.MESH
EMPTY = 1 << 20


def tables():
    f32 = np.float32
    index = np.arange(WIN)
    step = f32(2.0 * math.pi / WIN)

    def rounded(fn, phase):
        angle = (phase % WIN).astype(f32) * step
        return fn(angle.astype(np.float64)).astype(f32).astype(ml_dtypes.bfloat16).astype(f32)

    phase = index[:, None] * index[None, :]
    cosine, sine = rounded(np.cos, phase), rounded(np.sin, phase)
    back = (np.arange(SHIFTS) - RADIUS)[:, None] * index[None, :]
    back_cos, back_sin = rounded(np.cos, back), rounded(np.sin, back)

    right = np.zeros((PHASES, 256, 256), f32)
    for m in range(PHASES):
        rows = slice(32 * m, 32 * m + WIN)
        right[m, rows, :HALF] = cosine[:, :HALF]
        right[m, rows, 128 : 128 + HALF] = -sine[:, :HALF]
    order = np.concatenate([np.arange(QUARTER) * PHASES + m for m in range(PHASES)])
    c, s = cosine[:, order], sine[:, order]
    left = np.concatenate([np.concatenate([c, s], 1), np.concatenate([-s, c], 1)], 0)
    back_left = np.zeros((2 * QROWS, 2 * WIN), f32)
    back_left[:SHIFTS] = np.concatenate([back_cos, -back_sin], 1)
    back_left[QROWS : QROWS + SHIFTS] = np.concatenate([back_sin, back_cos], 1)
    weight = np.full(HALF, 2.0, f32)
    weight[0] = weight[-1] = 1.0
    back_right = np.zeros((512, 128), f32)
    energy = np.zeros((256, 128), f32)
    member = np.zeros((2, 8, 128), f32)
    for i in range(CAP):
        rows, lanes = HALF * i, TLANES * i
        back_right[rows : rows + HALF, lanes : lanes + SHIFTS] = weight[:, None] * back_cos[:, :HALF].T
        back_right[256 + rows : 256 + rows + HALF, lanes : lanes + SHIFTS] = (
            -weight[:, None] * back_sin[:, :HALF].T
        )
        energy[rows : rows + HALF, lanes : lanes + TLANES] = weight[:, None]
        member[0, i, lanes : lanes + SHIFTS] = 1.0
        member[1, CAP + i, lanes : lanes + SHIFTS] = 1.0
    return [jnp.asarray(t.astype(ml_dtypes.bfloat16)) for t in (right, left, back_left, back_right, energy, member)]


def split3(x):
    high = x.astype(BF16)
    rest = x - high.astype(F32)
    middle = rest.astype(BF16)
    low = (rest - middle.astype(F32)).astype(BF16)
    return high, middle, low


def exact_dot(x, table):
    rows = x.shape[0]
    out = jnp.dot(jnp.concatenate(split3(x), axis=0), table, preferred_element_type=F32)
    return out[:rows] + out[rows : 2 * rows] + out[2 * rows :]


def lane_iota(rows=1):
    return lax.broadcasted_iota(jnp.int32, (rows, 128), 1)


SECTION_RECV = (
    ((1, 0), (1, 1), (1, 2)),
    ((0, 3), (2, 0), (2, 1)),
    ((1, 2), (1, 3), (3, 0)),
    ((2, 1), (2, 2), (2, 3)),
)


STEPS = (
    (1, 0, 0), (1, 0, 1), (-1, 0, 1), (1, 0, 2), (0, 0, 1), (2, 0, -1), "y", (0, 0, 2),
    (-1, 1, 0), (-1, 1, -1), (1, 1, -1), (-1, 1, 2), (0, 1, -1), (2, 1, 1), "x", "xz",
)


def moved(me, step, sign):
    y, x, z = me // 8, me // 4 % 2, me % 4
    move = STEPS[step]
    if move == "y":
        upper = y // 2
        move = (2, 0, 2 * (1 - upper) if sign > 0 else 2 * upper)
    elif isinstance(move, str):
        move = (2 * (1 - x) if sign > 0 else 2 * x, 1, 2 if move == "xz" else 0)
    dy, dx, dz = move
    return (y + sign * dy + 4) % 4 * 8 + (x + dx) % 2 * 4 + (z + sign * dz + 4) % 4


def section_sends(section):
    return [
        (to, source, chunk)
        for to in range(SECTIONS)
        for chunk, (origin, source) in enumerate(SECTION_RECV[to])
        if origin == section
    ]


def flow_kernel(
    win_hbm, dev_ref, slot_ref,
    right_hbm, left_hbm, back_left_hbm, back_right_hbm, energy_hbm, member_hbm,
    out_ref,
    right_ref, left_ref, back_left_ref, back_right_ref, energy_ref, member_ref,
    win_ref, seg_re, seg_im, spectra, natural, outgoing, packed, from_section, from_region,
    cross, backs, squares, sums, dev_row, slot_row, ids_vmem, ids, local_ids,
    from_slot, from_group, from_partner, gathered, mine, field, fields,
    load_sem, ids_sem, sec_send, sec_recv, reg_send, reg_recv, p1_send, p1_recv, p2_send, p2_recv,
):
    me = lax.axis_index("region")
    sec = lax.axis_index("sec")

    def neighbour(o):
        return {"region": (me + o) % REGIONS}

    width = WIN * WIN // PARTS
    load_right = pltpu.make_async_copy(right_hbm, right_ref, load_sem.at[PARTS])
    load_tables = [
        pltpu.make_async_copy(source, into, load_sem.at[PARTS + 1 + k])
        for k, (source, into) in enumerate(
            (
                (left_hbm, left_ref),
                (back_left_hbm, back_left_ref),
                (back_right_hbm, back_right_ref),
                (energy_hbm, energy_ref),
                (member_hbm, member_ref),
            )
        )
    ]

    def load_part(part):
        lanes = pl.ds(part * width, width)
        return pltpu.make_async_copy(
            win_hbm.at[0, :, lanes], win_ref.at[:, lanes], load_sem.at[part]
        )

    load_right.start()
    for part in range(PARTS):
        load_part(part).start()
    for load in load_tables:
        load.start()

    barrier = pltpu.get_barrier_semaphore()

    def greet(o, _):
        pl.semaphore_signal(barrier, inc=1, device_id=neighbour(o), device_id_type=MESH)
        return 0

    lax.fori_loop(1, REGIONS, greet, 0)
    for d in range(1, SECTIONS):
        pl.semaphore_signal(
            barrier, inc=1, device_id={"sec": (sec + d) % SECTIONS}, device_id_type=MESH
        )

    lane = lane_iota()
    dev_row[...] = jnp.full((1, 128), -1, jnp.int32)
    slot_row[...] = jnp.full((1, 128), -1, jnp.int32)
    dev_row[0:1, 0:WIN_DEV] = dev_ref[...].reshape(1, WIN_DEV)
    slot_row[0:1, 0:WIN_DEV] = slot_ref[...].reshape(1, WIN_DEV)
    device, partner = dev_row[...], slot_row[...]
    code = jnp.where(me < device, lane, partner) * 64 + lane
    same = device == lax.broadcasted_iota(jnp.int32, (REGIONS, 128), 0)
    left_over = jnp.where(same, code, EMPTY)
    rank = jnp.zeros((1, 128), jnp.int32)
    listed = jnp.zeros((REGIONS, 128), jnp.int32)
    lane32 = lane_iota(REGIONS)
    for i in range(CAP):
        least = jnp.min(left_over, axis=1, keepdims=True)
        found = jnp.logical_and(same, left_over == least)
        rank += i * jnp.sum(jnp.where(found, 1, 0), axis=0, keepdims=True)
        window = jnp.where(least < EMPTY, least % 64, 0)
        listed = jnp.where(lane32 == i, window, listed)
        left_over = jnp.where(left_over > least, left_over, EMPTY)
    ids_vmem[...] = listed
    load_ids = pltpu.make_async_copy(ids_vmem, ids, ids_sem)
    load_ids.start()

    load_right.wait()
    for part in range(PARTS):
        load_part(part).wait()
        for m in range(PHASES):
            rows = [
                win_ref[:, 640 * q + 128 * m : 640 * q + 128 * m + 256]
                for q in range(8 * part, 8 * part + 8)
            ]
            seg = jnp.dot(
                jnp.concatenate(rows, axis=0), right_ref[m], preferred_element_type=F32
            )
            start = (QUARTER * m + 8 * part) * WIN_DEV
            seg_re[start : start + 8 * WIN_DEV, :] = seg[:, :128]
            seg_im[start : start + 8 * WIN_DEV, :] = seg[:, 128:]
    for load in load_tables:
        load.wait()
    load_ids.wait()
    for step in range(STEPS_DEV):
        origin = moved(me, step, -1)
        for i in range(CAP):
            local_ids[CAP * step + i] = ids[origin, i]

    wide = lane_iota(2 * WIN)

    def pack(windows):
        x0, x1, x2 = [spectra[w] for w in windows]
        x1 = pltpu.roll(x1, HALF, 1)
        x2 = pltpu.roll(x2, 2 * HALF - 128, 1)
        return jnp.concatenate(
            [jnp.where(wide < HALF, x0, x1), jnp.where(wide < 2 * HALF - 128, x1, x2)], axis=1
        )

    def section_copy(k, index):
        to, source, chunk = section_sends(k)[index]
        return pltpu.make_async_remote_copy(
            src_ref=natural.at[pl.ds(CHUNK * source, CHUNK)],
            dst_ref=from_section.at[pl.ds(CHUNK * chunk, CHUNK)],
            send_sem=sec_send.at[index],
            recv_sem=sec_recv.at[chunk],
            device_id={"sec": to},
            device_id_type=MESH,
        )

    def region_copy(step):
        to = moved(me, step, 1)
        return pltpu.make_async_remote_copy(
            src_ref=outgoing.at[step],
            dst_ref=from_region.at[step],
            send_sem=reg_send.at[step],
            recv_sem=reg_recv.at[step],
            device_id={"region": to},
            device_id_type=MESH,
        )

    def spectra_step(step, first):
        part = (2 * first + step) % (2 * QUARTERS)
        for pair in range(CAP):
            w = 2 * CAP * part + 2 * pair
            sides = [
                jnp.concatenate(
                    [seg[pl.ds(w + k, WIN, stride=WIN_DEV), :] for k in range(2)], axis=1
                ).astype(BF16)
                for seg in (seg_re, seg_im)
            ]
            spectrum = jnp.dot(
                left_ref[...], jnp.concatenate(sides, axis=0), preferred_element_type=F32
            ).astype(BF16)
            spectra[w] = spectrum[:, :128]
            spectra[w + 1] = spectrum[:, 128:]
        for k in range(2):
            w = 2 * CAP * part + CAP * k
            natural[2 * part + k] = pack([w, w + 1, w + 2])
        return first

    start = jnp.where(sec == 1, 2, 0)
    for quarter in range(QUARTERS):
        lax.fori_loop(2 * quarter, 2 * quarter + 2, spectra_step, start)
        if quarter == 0:
            pl.semaphore_wait(barrier, REGIONS - 1 + SECTIONS - 1)
        for k in range(SECTIONS):
            done = (quarter + (2 if k == 1 else 0)) % QUARTERS

            @pl.when(sec == k)
            def _():
                for index, (_, source, _) in enumerate(section_sends(k)):
                    if source == done:
                        section_copy(k, index).start()

    for step in list(range(STEPS_DEV // 2, STEPS_DEV)) + list(range(STEPS_DEV // 2)):
        to = moved(me, step, 1)
        outgoing[step] = pack([ids[to, i] for i in range(CAP)])
        region_copy(step).start()

    row = lax.broadcasted_iota(jnp.int32, (128, 128), 0)
    column = lax.broadcasted_iota(jnp.int32, (128, 128), 1)
    origin = jnp.full((128, 128), -2, jnp.int32)
    local = jnp.zeros((8, 128), jnp.bool_)
    for step in range(STEPS_DEV):
        origin = jnp.where(row == step, moved(me, step, -1), origin)
        local = jnp.logical_or(local, jnp.broadcast_to(device, (8, 128)) == moved(me, step, -1))
    for i in range(CAP):
        chosen = jnp.logical_and(origin == device, rank == i)
        from_slot[:, 128 * i : 128 * i + 128] = chosen.astype(F32).astype(BF16)
        chosen = CAP * row + i == column
        chosen = jnp.logical_and(chosen, column < WIN_DEV)
        from_group[:, 128 * i : 128 * i + 128] = chosen.astype(F32).astype(BF16)
    from_partner[...] = (row == partner).astype(F32).astype(BF16)

    sums[...] = jnp.zeros_like(sums)
    row_shift = lax.broadcasted_iota(jnp.int32, (QROWS, 128), 0)
    shift_mask = jnp.logical_and(row_shift < SHIFTS, lane_iota(QROWS) % TLANES < SHIFTS)
    row_value = (row_shift - RADIUS).astype(F32)

    def correlate(first_ref, second_ref, u):
        energy_a = jnp.zeros((8, 256), F32)
        energy_b = jnp.zeros((8, 256), F32)
        for r in range(0, WIN, 32):
            ar = first_ref[r : r + 32, :].astype(F32)
            ai = first_ref[WIN + r : WIN + r + 32, :].astype(F32)
            br = second_ref[r : r + 32, :].astype(F32)
            bi = second_ref[WIN + r : WIN + r + 32, :].astype(F32)
            scale = 1.0 / (WIN * WIN)
            cross[u, r : r + 32, :] = ((ar * br + ai * bi) * scale).astype(BF16)
            cross[u, WIN + r : WIN + r + 32, :] = ((ai * br - ar * bi) * scale).astype(BF16)
            energy_a += jnp.sum((ar * ar + ai * ai).reshape(4, 8, 256), axis=0)
            energy_b += jnp.sum((br * br + bi * bi).reshape(4, 8, 256), axis=0)
        squares[16 * u : 16 * u + 8, :] = energy_a
        squares[16 * u + 8 : 16 * u + 16, :] = energy_b
        back = jnp.dot(back_left_ref[...], cross[u], preferred_element_type=F32).astype(BF16)
        backs[QROWS * u : QROWS * u + QROWS, :256] = back[:QROWS]
        backs[QROWS * u : QROWS * u + QROWS, 256:] = back[QROWS:]

    def weigh(rows):
        surfaces = jnp.dot(backs[...], back_right_ref[...], preferred_element_type=F32)
        energies = exact_dot(squares[...], energy_ref[...]) / (WIN * WIN)
        for u, row in enumerate(rows):
            first = jnp.sum(energies[16 * u : 16 * u + 8], axis=0, keepdims=True)
            second = jnp.sum(energies[16 * u + 8 : 16 * u + 16], axis=0, keepdims=True)
            norm = jnp.sqrt(first * second + 1e-06)
            surface = surfaces[QROWS * u : QROWS * u + QROWS]
            weights = jnp.where(shift_mask, jnp.exp(sharpness * (surface / norm)), 0.0)
            sums[0, pl.ds(row, 1), :] = jnp.sum(weights, axis=0, keepdims=True)
            sums[1, pl.ds(row, 1), :] = jnp.sum(weights * row_value, axis=0, keepdims=True)

    def section_batch(chunk, _):
        pltpu.make_async_remote_copy(
            src_ref=natural.at[pl.ds(0, CHUNK)],
            dst_ref=from_section.at[pl.ds(CHUNK * chunk, CHUNK)],
            send_sem=sec_send.at[0],
            recv_sem=sec_recv.at[chunk],
            device_id={"sec": (sec + 1) % SECTIONS},
            device_id_type=MESH,
        ).wait_recv()
        first = CHUNK * ((SHARE // CHUNK * sec + chunk) % QUARTERS)
        for u in range(CHUNK):
            correlate(natural.at[first + u], from_section.at[CHUNK * chunk + u], u)
        weigh([STEPS_DEV + CHUNK * chunk + u for u in range(CHUNK)])
        return 0

    def region_batch(batch, _):
        for u in range(CHUNK):
            step = CHUNK * batch + u
            packed[u] = pack([local_ids[CAP * step + i] for i in range(CAP)])
            pltpu.make_async_remote_copy(
                src_ref=outgoing.at[0],
                dst_ref=from_region.at[step],
                send_sem=reg_send.at[step],
                recv_sem=reg_recv.at[step],
                device_id=neighbour(1),
                device_id_type=MESH,
            ).wait_recv()
            correlate(packed.at[u], from_region.at[step], u)
        weigh([CHUNK * batch + u for u in range(CHUNK)])
        return 0

    batches = STEPS_DEV // CHUNK
    lax.fori_loop(0, batches // 2, region_batch, 0)
    lax.fori_loop(0, SHARE // CHUNK, section_batch, 0)
    lax.fori_loop(batches // 2, batches, region_batch, 0)

    nt = (((1,), (1,)), ((), ()))

    def turned(table, x):
        parts = [
            lax.dot_general(table, part, nt, preferred_element_type=F32) for part in split3(x)
        ]
        return parts[0] + parts[1] + parts[2]

    column_value = (lane % TLANES - RADIUS).astype(F32)
    total = turned(member_ref[0] + member_ref[1], sums[0])
    moment = turned(member_ref[0], sums[1]) + turned(member_ref[1], sums[0] * column_value)
    flows = moment / jnp.where(total == 0.0, 1.0, total)
    lane8 = lane_iota(8)
    swapped = jnp.logical_and(lane8 >= STEPS_DEV, lane8 < STEPS_DEV + CHUNK * sec)
    flows = jnp.where(swapped, -flows, flows)
    flows = jnp.where(jnp.abs(flows) <= 2.0 * RADIUS, flows, 0.0)
    mine[...] = flows

    def p1_copy(d):
        return pltpu.make_async_remote_copy(
            src_ref=mine,
            dst_ref=gathered.at[d - 1],
            send_sem=p1_send.at[d - 1],
            recv_sem=p1_recv.at[d - 1],
            device_id={"sec": (sec + d) % SECTIONS},
            device_id_type=MESH,
        )

    for d in range(1, SECTIONS):
        p1_copy(d).start()
    for d in range(1, SECTIONS):
        p1_copy(d).wait_recv()
    blocks = []
    section = jnp.zeros((8, 128), F32)
    for k in range(SECTIONS):
        block = flows
        for d in range(1, SECTIONS):
            block = jnp.where((sec - k + SECTIONS) % SECTIONS == d, gathered[d - 1], block)
        blocks.append(block)
        turned_block = pltpu.roll(block, (SHARE * k - STEPS_DEV + 128) % 128, 1)
        here = jnp.logical_and(lane8 >= SHARE * k, lane8 < SHARE * k + SHARE)
        section = jnp.where(here, turned_block, section)

    def by_window(x, table):
        spread = exact_dot(x, table)
        rows = []
        for k in range(x.shape[0] // 8):
            for c in range(2):
                at = 8 * k + CAP * c
                rows.append(
                    sum(spread[at + i : at + i + 1, 128 * i : 128 * i + 128] for i in range(CAP))
                )
        return rows

    edges = [section] + [
        pltpu.roll(section, 128 - GROUPS * e, 1) for e in range(1, SECTIONS - 1)
    ]
    edges = [jnp.where(lane8 < GROUPS, edge, 0.0) for edge in edges]
    blocks = [jnp.where(lane8 < STEPS_DEV, block, 0.0) for block in blocks]
    montage_rows = by_window(jnp.concatenate(blocks, axis=0), from_slot[...])
    section_rows = by_window(jnp.concatenate(edges, axis=0), from_group[...])
    montage = jnp.concatenate(montage_rows, axis=0)
    section = jnp.concatenate(section_rows + [jnp.zeros((2, 128), F32)], axis=0)
    field[0:8, :] = montage
    field[8:16, :] = section

    def p2_copy(o):
        return pltpu.make_async_remote_copy(
            src_ref=field,
            dst_ref=fields.at[REGIONS - o],
            send_sem=p2_send.at[o - 1],
            recv_sem=p2_recv.at[REGIONS - 1 - o],
            device_id=neighbour(o),
            device_id_type=MESH,
        )

    def p2_start(o, _):
        p2_copy(o).start()
        return 0

    def p2_wait(o, _):
        p2_copy(o).wait_recv()
        return 0

    lax.fori_loop(1, REGIONS, p2_start, 0)
    lax.fori_loop(1, REGIONS, p2_wait, 0)

    theirs = exact_dot(fields[1:].reshape(16 * (REGIONS - 1), 128), from_partner[...])
    partner_field = jnp.zeros((16, 128), F32)
    for o in range(1, REGIONS):
        here = jnp.broadcast_to(device, (16, 128)) == (me + o) % REGIONS
        partner_field = jnp.where(here, theirs[16 * o - 16 : 16 * o], partner_field)
    montage = jnp.where(local, montage, -partner_field[:8])
    partner_section = partner_field[8:]

    row8 = lax.broadcasted_iota(jnp.int32, (8, 128), 0)
    has_next = jnp.where(row8 < 2 * (SECTIONS - 1), 1.0, 0.0)
    has_prev = jnp.where(row8 >= 2, 1.0, 0.0)
    disagreement = 2.0 * montage

    def before(x):
        return pltpu.roll(x, 2, 0)

    def after(x):
        return pltpu.roll(x, 6, 0)

    def relax(u, p, apart, flow, previous):
        gradient = (
            montage_stiffness * (2.0 * u - 2.0 * p - apart)
            + section_stiffness * has_next * (u - after(u) - flow)
            - section_stiffness * has_prev * (before(u) - u - previous)
            + anchor_stiffness * u
        )
        return u - step_length * gradient

    previous, partner_previous = before(section), before(partner_section)

    def turn(_, state):
        u, p = state
        return (
            relax(u, p, disagreement, section, previous),
            relax(p, u, -disagreement, partner_section, partner_previous),
        )

    zero = jnp.zeros((8, 128), F32)
    shift, _ = lax.fori_loop(0, ITERS, turn, (zero, zero))
    for k, values in enumerate((montage, section, shift)):
        chosen = values[0:2]
        for n in range(1, SECTIONS):
            chosen = jnp.where(sec == n, values[2 * n : 2 * n + 2], chosen)
        out_ref[2 * k : 2 * k + 2, :] = chosen
    out_ref[6:8, :] = jnp.zeros((2, 128), F32)

    for k in range(SECTIONS):

        @pl.when(sec == k)
        def _():
            for index in range(len(section_sends(k))):
                section_copy(k, index).wait_send()

    for step in range(STEPS_DEV):
        region_copy(step).wait_send()
    for d in range(1, SECTIONS):
        p1_copy(d).wait_send()

    def p2_sent(o, _):
        p2_copy(o).wait_send()
        return 0

    lax.fori_loop(1, REGIONS, p2_sent, 0)


def split_kernel(rows_ref, montage_ref, section_ref, shift_ref):
    for k, ref in enumerate((montage_ref, section_ref, shift_ref)):
        ref[0] = rows_ref[2 * k : 2 * k + 2, :WIN_DEV]


VMEM = pl.BlockSpec(memory_space=pltpu.VMEM)
ANY = pl.BlockSpec(memory_space=pl.ANY)


def body(windows, partner_dev, partner_slot):
    side = (2 * WIN, 256)
    dma = pltpu.SemaphoreType.DMA
    rows = pl.pallas_call(
        flow_kernel,
        out_shape=jax.ShapeDtypeStruct((8, 128), F32),
        in_specs=[ANY, VMEM, VMEM] + [ANY] * 6,
        out_specs=VMEM,
        scratch_shapes=[
            pltpu.VMEM((PHASES, 256, 256), BF16),
            pltpu.VMEM((2 * WIN, 2 * WIN), BF16),
            pltpu.VMEM((2 * QROWS, 2 * WIN), BF16),
            pltpu.VMEM((512, 128), BF16),
            pltpu.VMEM((256, 128), BF16),
            pltpu.VMEM((2, 8, 128), BF16),
            pltpu.VMEM((WIN_DEV, WIN * WIN), BF16),
            pltpu.VMEM((WIN * WIN_DEV, 128), F32),
            pltpu.VMEM((WIN * WIN_DEV, 128), F32),
            pltpu.VMEM((WIN_DEV, 2 * WIN, 128), BF16),
            pltpu.VMEM((GROUPS,) + side, BF16),
            pltpu.VMEM((STEPS_DEV,) + side, BF16),
            pltpu.VMEM((CHUNK,) + side, BF16),
            pltpu.VMEM((SHARE,) + side, BF16),
            pltpu.VMEM((STEPS_DEV,) + side, BF16),
            pltpu.VMEM((CHUNK,) + side, BF16),
            pltpu.VMEM((CHUNK * QROWS, 512), BF16),
            pltpu.VMEM((CHUNK * 16, 256), F32),
            pltpu.VMEM((2, 128, 128), F32),
            pltpu.VMEM((1, 128), jnp.int32),
            pltpu.VMEM((1, 128), jnp.int32),
            pltpu.VMEM((REGIONS, 128), jnp.int32),
            pltpu.SMEM((REGIONS, 128), jnp.int32),
            pltpu.SMEM((CAP * STEPS_DEV,), jnp.int32),
            pltpu.VMEM((128, CAP * 128), BF16),
            pltpu.VMEM((128, CAP * 128), BF16),
            pltpu.VMEM((128, 128), BF16),
            pltpu.VMEM((SECTIONS - 1, 8, 128), F32),
            pltpu.VMEM((8, 128), F32),
            pltpu.VMEM((16, 128), F32),
            pltpu.VMEM((REGIONS, 16, 128), F32),
            dma((PARTS + 6,)),
            dma,
            dma((5,)),
            dma((SHARE // CHUNK,)),
            dma((STEPS_DEV,)),
            dma((STEPS_DEV,)),
            dma((SECTIONS - 1,)),
            dma((SECTIONS - 1,)),
            dma((REGIONS - 1,)),
            dma((REGIONS - 1,)),
        ],
        compiler_params=pltpu.CompilerParams(
            vmem_limit_bytes=60 << 20, collective_id=0, has_side_effects=True
        ),
        name="flows",
    )(windows, partner_dev, partner_slot, *tables())
    out = jax.ShapeDtypeStruct((1, 2, WIN_DEV), F32)
    return pl.pallas_call(
        split_kernel,
        out_shape=(out, out, out),
        in_specs=[VMEM],
        out_specs=(VMEM, VMEM, VMEM),
        name="split",
    )(rows)


def solution(mesh):
    placed = (P("sec", "region", None), P("region"), P("region"))
    return jax.shard_map(
        body,
        mesh=mesh,
        in_specs=placed,
        out_specs=(P("sec", None, "region"),) * 3,
        check_vma=False,
    )
```

```python
import functools
import math

import jax
import jax.numpy as jnp
import ml_dtypes
import numpy as np
from jax import lax
from jax.experimental import pallas as pl
from jax.experimental.pallas import tpu as pltpu
from jax.sharding import PartitionSpec as P

WIN = 160
RADIUS = 16
SHIFTS = 33
ITERS = 32
HALF = WIN // 2 + 1
CAP = 3
REGIONS = 32
SECTIONS = 4
WIN_DEV = 48
GROUPS = WIN_DEV // CAP
SHARE = 12
CHUNK = 4
QROWS = 48
TLANES = 40
PHASES = 4
QUARTER = WIN // PHASES
PARTS = 5
STEPS_DEV = REGIONS // 2
EARLY = STEPS_DEV - CHUNK
QUARTERS = GROUPS // CHUNK

sharpness = 12.0
montage_stiffness = 1.0
section_stiffness = 1.0
anchor_stiffness = 0.05
step_length = 0.2

F32 = jnp.float32
BF16 = jnp.bfloat16
MESH = pl.DeviceIdType.MESH
EMPTY = 1 << 20


def tables():
    f32 = np.float32
    index = np.arange(WIN)
    step = f32(2.0 * math.pi / WIN)

    def rounded(fn, phase):
        angle = (phase % WIN).astype(f32) * step
        return fn(angle.astype(np.float64)).astype(f32).astype(ml_dtypes.bfloat16).astype(f32)

    phase = index[:, None] * index[None, :]
    cosine, sine = rounded(np.cos, phase), rounded(np.sin, phase)
    back = (np.arange(SHIFTS) - RADIUS)[:, None] * index[None, :]
    back_cos, back_sin = rounded(np.cos, back), rounded(np.sin, back)

    right = np.zeros((PHASES, 256, 256), f32)
    for m in range(PHASES):
        rows = slice(32 * m, 32 * m + WIN)
        right[m, rows, :HALF] = cosine[:, :HALF]
        right[m, rows, 128 : 128 + HALF] = -sine[:, :HALF]
    order = np.concatenate([np.arange(QUARTER) * PHASES + m for m in range(PHASES)])
    c, s = cosine[:, order], sine[:, order]
    left = np.concatenate([np.concatenate([c, s], 1), np.concatenate([-s, c], 1)], 0)
    back_left = np.zeros((2 * QROWS, 2 * WIN), f32)
    back_left[:SHIFTS] = np.concatenate([back_cos, -back_sin], 1)
    back_left[QROWS : QROWS + SHIFTS] = np.concatenate([back_sin, back_cos], 1)
    weight = np.full(HALF, 2.0, f32)
    weight[0] = weight[-1] = 1.0
    back_right = np.zeros((512, 128), f32)
    energy = np.zeros((256, 128), f32)
    member = np.zeros((8, 128), f32)
    for i in range(CAP):
        rows, lanes = HALF * i, TLANES * i
        back_right[rows : rows + HALF, lanes : lanes + SHIFTS] = weight[:, None] * back_cos[:, :HALF].T
        back_right[256 + rows : 256 + rows + HALF, lanes : lanes + SHIFTS] = (
            -weight[:, None] * back_sin[:, :HALF].T
        )
        energy[rows : rows + HALF, lanes : lanes + TLANES] = weight[:, None]
        member[i::CAP, lanes : lanes + SHIFTS] = 1.0
    member[2 * CAP :] = 0.0
    return [jnp.asarray(t.astype(ml_dtypes.bfloat16)) for t in (right, left, back_left, back_right, energy, member)]


def split3(x):
    high = x.astype(BF16)
    rest = x - high.astype(F32)
    middle = rest.astype(BF16)
    low = (rest - middle.astype(F32)).astype(BF16)
    return high, middle, low


def exact_dot(x, table):
    rows = x.shape[0]
    out = jnp.dot(jnp.concatenate(split3(x), axis=0), table, preferred_element_type=F32)
    return out[:rows] + out[rows : 2 * rows] + out[2 * rows :]


def lane_iota(rows=1):
    return lax.broadcasted_iota(jnp.int32, (rows, 128), 1)


SECTION_RECV = (
    ((1, 0), (1, 1), (1, 2)),
    ((0, 3), (2, 0), (2, 1)),
    ((1, 2), (1, 3), (3, 0)),
    ((2, 1), (2, 2), (2, 3)),
)


STEPS = (
    (1, 0, 0), (1, 0, 1), (-1, 0, 1), (1, 0, 2), (0, 0, 1), (2, 0, -1), "y", (0, 0, 2),
    (-1, 1, 0), (-1, 1, -1), (1, 1, -1), (-1, 1, 2), (0, 1, -1), (2, 1, 1), "x", "xz",
)
MUTUAL = STEPS.index((0, 0, 2))


def moved(me, step, sign):
    y, x, z = me // 8, me // 4 % 2, me % 4
    move = STEPS[step]
    if move == "y":
        upper = y // 2
        move = (2, 0, 2 * (1 - upper) if sign > 0 else 2 * upper)
    elif isinstance(move, str):
        move = (2 * (1 - x) if sign > 0 else 2 * x, 1, 2 if move == "xz" else 0)
    dy, dx, dz = move
    return (y + sign * dy + 4) % 4 * 8 + (x + dx) % 2 * 4 + (z + sign * dz + 4) % 4


def section_sends(section):
    return [
        (to, source, chunk)
        for to in range(SECTIONS)
        for chunk, (origin, source) in enumerate(SECTION_RECV[to])
        if origin == section
    ]


def flow_kernel(
    win_hbm, dev_ref, slot_ref,
    right_hbm, left_hbm, back_left_hbm, back_right_hbm, energy_hbm, member_hbm,
    out_ref,
    right_ref, left_ref, back_left_ref, back_right_ref, energy_ref, member_ref,
    win_ref, seg_re, seg_im, spectra, natural, outgoing, packed, from_section, from_region,
    cross, backs, squares, sums, dev_row, slot_row, ids_vmem, ids,
    from_slot, from_group, from_partner, published, ours, early, late, sections, field, fields,
    load_sem, ids_sem, sec_send, sec_recv, reg_send, reg_recv,
    field_send, field_recv, ours_send, ours_recv, early_send, early_recv, late_send, late_recv, ready,
):
    me = lax.axis_index("region")
    sec = lax.axis_index("sec")

    def neighbour(o):
        return {"region": (me + o) % REGIONS}

    barrier = pltpu.get_barrier_semaphore()

    def greet(o, _):
        pl.semaphore_signal(barrier, inc=1, device_id=neighbour(o), device_id_type=MESH)
        return 0

    lax.fori_loop(1, REGIONS, greet, 0)
    for d in range(1, SECTIONS):
        pl.semaphore_signal(
            barrier, inc=1, device_id={"sec": (sec + d) % SECTIONS}, device_id_type=MESH
        )

    width = WIN * WIN // PARTS
    load_right = pltpu.make_async_copy(right_hbm, right_ref, load_sem.at[PARTS])
    load_tables = [
        pltpu.make_async_copy(source, into, load_sem.at[PARTS + 1 + k])
        for k, (source, into) in enumerate(
            (
                (left_hbm, left_ref),
                (back_left_hbm, back_left_ref),
                (back_right_hbm, back_right_ref),
                (energy_hbm, energy_ref),
                (member_hbm, member_ref),
            )
        )
    ]

    def load_part(part):
        lanes = pl.ds(part * width, width)
        return pltpu.make_async_copy(
            win_hbm.at[0, :, lanes], win_ref.at[:, lanes], load_sem.at[part]
        )

    load_right.start()
    for part in range(PARTS):
        load_part(part).start()
    for load in load_tables:
        load.start()

    lane = lane_iota()
    dev_row[...] = jnp.full((1, 128), -1, jnp.int32)
    slot_row[...] = jnp.full((1, 128), -1, jnp.int32)
    dev_row[0:1, 0:WIN_DEV] = dev_ref[...].reshape(1, WIN_DEV)
    slot_row[0:1, 0:WIN_DEV] = slot_ref[...].reshape(1, WIN_DEV)
    device, partner = dev_row[...], slot_row[...]
    code = jnp.where(me < device, lane, partner) * 64 + lane
    same = device == lax.broadcasted_iota(jnp.int32, (REGIONS, 128), 0)
    left_over = jnp.where(same, code, EMPTY)
    rank = jnp.zeros((1, 128), jnp.int32)
    listed = jnp.zeros((REGIONS, 128), jnp.int32)
    lane32 = lane_iota(REGIONS)
    for i in range(CAP):
        least = jnp.min(left_over, axis=1, keepdims=True)
        found = jnp.logical_and(same, left_over == least)
        rank += i * jnp.sum(jnp.where(found, 1, 0), axis=0, keepdims=True)
        window = jnp.where(least < EMPTY, least % 64, 0)
        listed = jnp.where(lane32 == i, window, listed)
        left_over = jnp.where(left_over > least, left_over, EMPTY)
    ids_vmem[...] = listed
    load_ids = pltpu.make_async_copy(ids_vmem, ids, ids_sem)
    load_ids.start()

    load_right.wait()
    for part in range(PARTS):
        load_part(part).wait()
        for m in range(PHASES):
            rows = [
                win_ref[:, 640 * q + 128 * m : 640 * q + 128 * m + 256]
                for q in range(8 * part, 8 * part + 8)
            ]
            seg = jnp.dot(
                jnp.concatenate(rows, axis=0), right_ref[m], preferred_element_type=F32
            )
            start = (QUARTER * m + 8 * part) * WIN_DEV
            seg_re[start : start + 8 * WIN_DEV, :] = seg[:, :128]
            seg_im[start : start + 8 * WIN_DEV, :] = seg[:, 128:]
    for load in load_tables:
        load.wait()
    load_ids.wait()

    wide = lane_iota(2 * WIN)

    def pack(windows):
        x0, x1, x2 = [spectra[w] for w in windows]
        x1 = pltpu.roll(x1, HALF, 1)
        x2 = pltpu.roll(x2, 2 * HALF - 128, 1)
        return jnp.concatenate(
            [jnp.where(wide < HALF, x0, x1), jnp.where(wide < 2 * HALF - 128, x1, x2)], axis=1
        )

    def section_copy(k, index):
        to, source, chunk = section_sends(k)[index]
        return pltpu.make_async_remote_copy(
            src_ref=natural.at[pl.ds(CHUNK * source, CHUNK)],
            dst_ref=from_section.at[pl.ds(CHUNK * chunk, CHUNK)],
            send_sem=sec_send.at[index],
            recv_sem=sec_recv.at[chunk],
            device_id={"sec": to},
            device_id_type=MESH,
        )

    def region_copy(step):
        to = moved(me, step, 1)
        return pltpu.make_async_remote_copy(
            src_ref=outgoing.at[step],
            dst_ref=from_region.at[step],
            send_sem=reg_send.at[step],
            recv_sem=reg_recv.at[step],
            device_id={"region": to},
            device_id_type=MESH,
        )

    def spectra_step(step, first):
        part = (2 * first + step) % (2 * QUARTERS)
        for pair in range(CAP):
            w = 2 * CAP * part + 2 * pair
            sides = [
                jnp.concatenate(
                    [seg[pl.ds(w + k, WIN, stride=WIN_DEV), :] for k in range(2)], axis=1
                ).astype(BF16)
                for seg in (seg_re, seg_im)
            ]
            spectrum = jnp.dot(
                left_ref[...], jnp.concatenate(sides, axis=0), preferred_element_type=F32
            ).astype(BF16)
            spectra[w] = spectrum[:, :128]
            spectra[w + 1] = spectrum[:, 128:]
        for k in range(2):
            w = 2 * CAP * part + CAP * k
            natural[2 * part + k] = pack([w, w + 1, w + 2])
        return first

    start = jnp.where(sec == 1, 2, 0)
    for quarter in range(QUARTERS):
        lax.fori_loop(2 * quarter, 2 * quarter + 2, spectra_step, start)
        if quarter == 0:
            pl.semaphore_wait(barrier, REGIONS - 1 + SECTIONS - 1)
            for d in range(1, SECTIONS):
                pl.semaphore_signal(
                    ready, inc=1, device_id={"sec": (sec + d) % SECTIONS}, device_id_type=MESH
                )
        for k in range(SECTIONS):
            done = (quarter + (2 if k == 1 else 0)) % QUARTERS

            @pl.when(sec == k)
            def _():
                for index, (_, source, _) in enumerate(section_sends(k)):
                    if source == done:
                        section_copy(k, index).start()

    for step in range(STEPS_DEV):
        to = moved(me, step, 1)
        outgoing[step] = pack([ids[to, i] for i in range(CAP)])
        region_copy(step).start()

    row = lax.broadcasted_iota(jnp.int32, (128, 128), 0)
    column = lax.broadcasted_iota(jnp.int32, (128, 128), 1)
    origin = jnp.full((128, 128), -2, jnp.int32)
    for step in range(STEPS_DEV):
        origin = jnp.where(row == step, moved(me, step, -1), origin)
        if step != MUTUAL:
            origin = jnp.where(row == STEPS_DEV + step, moved(me, step, 1), origin)
    sign = jnp.where(row < STEPS_DEV, 1.0, -1.0)
    for i in range(CAP):
        chosen = jnp.logical_and(origin == device, rank == i)
        from_slot[:, 128 * i : 128 * i + 128] = jnp.where(chosen, sign, 0.0).astype(BF16)
        chosen = CAP * row + i == column
        chosen = jnp.logical_and(chosen, column < WIN_DEV)
        from_group[:, 128 * i : 128 * i + 128] = chosen.astype(F32).astype(BF16)
    from_partner[...] = (row == partner).astype(F32).astype(BF16)

    sums[...] = jnp.zeros_like(sums)
    row_shift = lax.broadcasted_iota(jnp.int32, (QROWS, 128), 0)
    shift_mask = jnp.logical_and(row_shift < SHIFTS, lane_iota(QROWS) % TLANES < SHIFTS)
    row_value = (row_shift - RADIUS).astype(F32)

    def correlate(first_ref, second_ref, u):
        energy_a = jnp.zeros((8, 256), F32)
        energy_b = jnp.zeros((8, 256), F32)
        for r in range(0, WIN, 32):
            ar = first_ref[r : r + 32, :].astype(F32)
            ai = first_ref[WIN + r : WIN + r + 32, :].astype(F32)
            br = second_ref[r : r + 32, :].astype(F32)
            bi = second_ref[WIN + r : WIN + r + 32, :].astype(F32)
            scale = 1.0 / (WIN * WIN)
            cross[u, r : r + 32, :] = ((ar * br + ai * bi) * scale).astype(BF16)
            cross[u, WIN + r : WIN + r + 32, :] = ((ai * br - ar * bi) * scale).astype(BF16)
            energy_a += jnp.sum((ar * ar + ai * ai).reshape(4, 8, 256), axis=0)
            energy_b += jnp.sum((br * br + bi * bi).reshape(4, 8, 256), axis=0)
        squares[16 * u : 16 * u + 8, :] = energy_a
        squares[16 * u + 8 : 16 * u + 16, :] = energy_b
        back = jnp.dot(back_left_ref[...], cross[u], preferred_element_type=F32).astype(BF16)
        backs[QROWS * u : QROWS * u + QROWS, :256] = back[:QROWS]
        backs[QROWS * u : QROWS * u + QROWS, 256:] = back[QROWS:]

    column_value = (lane % TLANES - RADIUS).astype(F32)
    lane8 = lane_iota(8)
    row8 = lax.broadcasted_iota(jnp.int32, (8, 128), 0)

    def weigh():
        surfaces = jnp.dot(backs[...], back_right_ref[...], preferred_element_type=F32)
        energies = exact_dot(squares[...], energy_ref[...]) / (WIN * WIN)
        for u in range(CHUNK):
            first = jnp.sum(energies[16 * u : 16 * u + 8], axis=0, keepdims=True)
            second = jnp.sum(energies[16 * u + 8 : 16 * u + 16], axis=0, keepdims=True)
            norm = jnp.sqrt(first * second + 1e-06)
            surface = surfaces[QROWS * u : QROWS * u + QROWS]
            weights = jnp.where(shift_mask, jnp.exp(sharpness * (surface / norm)), 0.0)
            total = jnp.sum(weights, axis=0, keepdims=True)
            sums[u : u + 1, :] = total
            sums[8 + u : 9 + u, :] = jnp.sum(weights * row_value, axis=0, keepdims=True)
            sums[16 + u : 17 + u, :] = total * column_value
        parts = [
            lax.dot_general(
                member_ref[...], part, (((1,), (1,)), ((), ())), preferred_element_type=F32
            )
            for part in split3(sums[...])
        ]
        total = parts[0] + parts[1] + parts[2]
        moment = jnp.where(row8 < CAP, pltpu.roll(total, 128 - 8, 1), pltpu.roll(total, 128 - 16, 1))
        flows = moment / jnp.where(total == 0.0, 1.0, total)
        return jnp.where(jnp.logical_and(jnp.abs(flows) <= 2.0 * RADIUS, lane8 < CHUNK), flows, 0.0)

    def section_batch(chunk, _):
        pltpu.make_async_remote_copy(
            src_ref=natural.at[pl.ds(0, CHUNK)],
            dst_ref=from_section.at[pl.ds(CHUNK * chunk, CHUNK)],
            send_sem=sec_send.at[0],
            recv_sem=sec_recv.at[chunk],
            device_id={"sec": (sec + 1) % SECTIONS},
            device_id_type=MESH,
        ).wait_recv()
        first = CHUNK * ((SHARE // CHUNK * sec + chunk) % QUARTERS)
        for u in range(CHUNK):
            correlate(natural.at[first + u], from_section.at[CHUNK * chunk + u], u)
        flows = weigh()
        flows = jnp.where(chunk < sec, -flows, flows)
        sections[...] += pltpu.roll(flows, CHUNK * chunk, 1)
        return 0

    def early_copy(step):
        return pltpu.make_async_remote_copy(
            src_ref=published.at[0],
            dst_ref=early.at[step],
            send_sem=early_send,
            recv_sem=early_recv,
            device_id={"region": moved(me, step, -1)},
            device_id_type=MESH,
        )

    def late_copy(step, k):
        return pltpu.make_async_remote_copy(
            src_ref=published.at[1],
            dst_ref=late.at[step - EARLY, sec],
            send_sem=late_send,
            recv_sem=late_recv,
            device_id={"sec": k, "region": moved(me, step, -1)},
            device_id_type=MESH,
        )

    def ours_copy(d):
        return pltpu.make_async_remote_copy(
            src_ref=ours.at[0],
            dst_ref=ours.at[d],
            send_sem=ours_send,
            recv_sem=ours_recv,
            device_id={"sec": (sec + d) % SECTIONS},
            device_id_type=MESH,
        )

    def field_copy(o):
        return pltpu.make_async_remote_copy(
            src_ref=field,
            dst_ref=fields.at[REGIONS - 1 - o],
            send_sem=field_send,
            recv_sem=field_recv,
            device_id=neighbour(o),
            device_id_type=MESH,
        )

    def region_batch(batch):
        for u in range(CHUNK):
            step = CHUNK * batch + u
            origin = moved(me, step, -1)
            packed[u] = pack([ids[origin, i] for i in range(CAP)])
            region_copy(step).wait_recv()
            correlate(packed.at[u], from_region.at[step], u)
        flows = weigh()
        flows += pltpu.roll(flows, STEPS_DEV, 1)
        return pltpu.roll(flows, CHUNK * batch, 1) if batch else flows

    def by_window(x, table):
        spread = exact_dot(x, table)
        rows = []
        for k in range(x.shape[0] // 8):
            for c in range(2):
                at = 8 * k + CAP * c
                rows.append(
                    sum(spread[at + i : at + i + 1, 128 * i : 128 * i + 128] for i in range(CAP))
                )
        return rows

    sections[...] = jnp.zeros((8, 128), F32)
    flows = region_batch(0) + region_batch(1)
    lax.fori_loop(0, SHARE // CHUNK, section_batch, 0)
    section = sections[...]
    shift = section
    for k in range(1, SECTIONS):
        shift = jnp.where(sec == k, pltpu.roll(section, SHARE * k, 1), shift)
    edges = [shift] + [pltpu.roll(shift, 128 - GROUPS * e, 1) for e in range(1, SECTIONS - 1)]
    edges = [jnp.where(lane8 < GROUPS, edge, 0.0) for edge in edges]
    section_rows = by_window(jnp.concatenate(edges, axis=0), from_group[...])
    section = jnp.concatenate(section_rows + [jnp.zeros((2, 128), F32)], axis=0)
    field[...] = section

    def field_start(o, _):
        field_copy(o).start()
        return 0

    lax.fori_loop(1, REGIONS, field_start, 0)
    pl.semaphore_wait(ready, SECTIONS - 1)
    flows += region_batch(2)
    published[0] = flows
    for step in range(EARLY):
        early_copy(step).start()
    flows += region_batch(3)
    published[1] = flows
    for step in range(EARLY, STEPS_DEV):
        for k in range(SECTIONS):
            late_copy(step, k).start()

    pltpu.make_async_copy(fields, fields, field_recv).wait()
    found = exact_dot(fields[...].reshape(8 * (REGIONS - 1), 128), from_partner[...])
    partner_section = jnp.zeros((8, 128), F32)
    for o in range(1, REGIONS):
        here = jnp.broadcast_to(device, (8, 128)) == (me + o) % REGIONS
        partner_section = jnp.where(here, found[8 * o - 8 : 8 * o], partner_section)
    pltpu.make_async_copy(early, early, early_recv).wait()
    for step in range(EARLY):
        flows = jnp.where(lane8 == STEPS_DEV + step, early[step], flows)
    ours[0, 0:8, :] = flows
    ours[0, 8:16, :] = section
    ours[0, 16:24, :] = partner_section
    for d in range(1, SECTIONS):
        ours_copy(d).start()
    for k in range(SECTIONS):

        @pl.when(sec == k)
        def _():
            for index in range(len(section_sends(k))):
                section_copy(k, index).wait_send()

    for step in range(STEPS_DEV):
        region_copy(step).wait_send()
    pltpu.make_async_copy(fields, fields, field_send).wait()
    pltpu.make_async_copy(early, early, early_send).wait()
    pltpu.make_async_copy(late, late, late_recv).wait()
    others = ours.at[pl.ds(1, SECTIONS - 1)]
    pltpu.make_async_copy(others, others, ours_recv).wait()
    blocks = []
    for k in range(SECTIONS):
        block = ours[(sec - k + SECTIONS) % SECTIONS, 0:8, :]
        for step in range(EARLY, STEPS_DEV):
            block = jnp.where(lane8 == STEPS_DEV + step, late[step - EARLY, k], block)
        blocks.append(block)
    montage = jnp.concatenate(
        by_window(jnp.concatenate(blocks, axis=0), from_slot[...]), axis=0
    )
    section = ours[0, 8:16, :] + ours[1, 8:16, :] + ours[2, 8:16, :] + ours[3, 8:16, :]
    partner_section = ours[0, 16:24, :] + ours[1, 16:24, :] + ours[2, 16:24, :] + ours[3, 16:24, :]

    has_next = jnp.where(row8 < 2 * (SECTIONS - 1), 1.0, 0.0)
    has_prev = jnp.where(row8 >= 2, 1.0, 0.0)
    disagreement = 2.0 * montage

    def before(x):
        return pltpu.roll(x, 2, 0)

    def after(x):
        return pltpu.roll(x, 6, 0)

    def relax(u, p, apart, flow, previous):
        gradient = (
            montage_stiffness * (2.0 * u - 2.0 * p - apart)
            + section_stiffness * has_next * (u - after(u) - flow)
            - section_stiffness * has_prev * (before(u) - u - previous)
            + anchor_stiffness * u
        )
        return u - step_length * gradient

    previous, partner_previous = before(section), before(partner_section)

    def turn(_, state):
        u, p = state
        return (
            relax(u, p, disagreement, section, previous),
            relax(p, u, -disagreement, partner_section, partner_previous),
        )

    zero = jnp.zeros((8, 128), F32)
    shift, _ = lax.fori_loop(0, ITERS, turn, (zero, zero))
    for k, values in enumerate((montage, section, shift)):
        chosen = values[0:2]
        for n in range(1, SECTIONS):
            chosen = jnp.where(sec == n, values[2 * n : 2 * n + 2], chosen)
        out_ref[2 * k : 2 * k + 2, :] = chosen
    out_ref[6:8, :] = jnp.zeros((2, 128), F32)

    pltpu.make_async_copy(late, late, late_send).wait()
    pltpu.make_async_copy(others, others, ours_send).wait()


def split_kernel(rows_ref, montage_ref, section_ref, shift_ref):
    for k, ref in enumerate((montage_ref, section_ref, shift_ref)):
        ref[0] = rows_ref[2 * k : 2 * k + 2, :WIN_DEV]


VMEM = pl.BlockSpec(memory_space=pltpu.VMEM)
ANY = pl.BlockSpec(memory_space=pl.ANY)


def body(windows, partner_dev, partner_slot):
    side = (2 * WIN, 256)
    dma = pltpu.SemaphoreType.DMA
    rows = pl.pallas_call(
        flow_kernel,
        out_shape=jax.ShapeDtypeStruct((8, 128), F32),
        in_specs=[ANY, VMEM, VMEM] + [ANY] * 6,
        out_specs=VMEM,
        scratch_shapes=[
            pltpu.VMEM((PHASES, 256, 256), BF16),
            pltpu.VMEM((2 * WIN, 2 * WIN), BF16),
            pltpu.VMEM((2 * QROWS, 2 * WIN), BF16),
            pltpu.VMEM((512, 128), BF16),
            pltpu.VMEM((256, 128), BF16),
            pltpu.VMEM((8, 128), BF16),
            pltpu.VMEM((WIN_DEV, WIN * WIN), BF16),
            pltpu.VMEM((WIN * WIN_DEV, 128), F32),
            pltpu.VMEM((WIN * WIN_DEV, 128), F32),
            pltpu.VMEM((WIN_DEV, 2 * WIN, 128), BF16),
            pltpu.VMEM((GROUPS,) + side, BF16),
            pltpu.VMEM((STEPS_DEV,) + side, BF16),
            pltpu.VMEM((CHUNK,) + side, BF16),
            pltpu.VMEM((SHARE,) + side, BF16),
            pltpu.VMEM((STEPS_DEV,) + side, BF16),
            pltpu.VMEM((CHUNK,) + side, BF16),
            pltpu.VMEM((CHUNK * QROWS, 512), BF16),
            pltpu.VMEM((CHUNK * 16, 256), F32),
            pltpu.VMEM((128, 128), F32),
            pltpu.VMEM((1, 128), jnp.int32),
            pltpu.VMEM((1, 128), jnp.int32),
            pltpu.VMEM((REGIONS, 128), jnp.int32),
            pltpu.SMEM((REGIONS, 128), jnp.int32),
            pltpu.VMEM((128, CAP * 128), BF16),
            pltpu.VMEM((128, CAP * 128), BF16),
            pltpu.VMEM((128, 128), BF16),
            pltpu.VMEM((2, 8, 128), F32),
            pltpu.VMEM((SECTIONS, 24, 128), F32),
            pltpu.VMEM((EARLY, 8, 128), F32),
            pltpu.VMEM((STEPS_DEV - EARLY, SECTIONS, 8, 128), F32),
            pltpu.VMEM((8, 128), F32),
            pltpu.VMEM((8, 128), F32),
            pltpu.VMEM((REGIONS - 1, 8, 128), F32),
            dma((PARTS + 6,)),
            dma,
            dma((5,)),
            dma((SHARE // CHUNK,)),
            dma((STEPS_DEV,)),
            dma((STEPS_DEV,)),
            dma,
            dma,
            dma,
            dma,
            dma,
            dma,
            dma,
            dma,
            pltpu.SemaphoreType.REGULAR,
        ],
        compiler_params=pltpu.CompilerParams(
            vmem_limit_bytes=60 << 20, collective_id=0, has_side_effects=True
        ),
        name="flows",
    )(windows, partner_dev, partner_slot, *tables())
    out = jax.ShapeDtypeStruct((1, 2, WIN_DEV), F32)
    return pl.pallas_call(
        split_kernel,
        out_shape=(out, out, out),
        in_specs=[VMEM],
        out_specs=(VMEM, VMEM, VMEM),
        name="split",
    )(rows)


def solution(mesh):
    placed = (P("sec", "region", None), P("region"), P("region"))
    return jax.shard_map(
        body,
        mesh=mesh,
        in_specs=placed,
        out_specs=(P("sec", None, "region"),) * 3,
        check_vma=False,
    )
```

```python
import functools
import math

import jax
import jax.numpy as jnp
import ml_dtypes
import numpy as np
from jax import lax
from jax.experimental import pallas as pl
from jax.experimental.pallas import tpu as pltpu
from jax.sharding import PartitionSpec as P

WIN = 160
RADIUS = 16
SHIFTS = 33
ITERS = 32
HALF = WIN // 2 + 1
CAP = 3
REGIONS = 32
SECTIONS = 4
WIN_DEV = 48
GROUPS = WIN_DEV // CAP
SHARE = 12
CHUNK = 4
QROWS = 48
TLANES = 40
PHASES = 4
QUARTER = WIN // PHASES
PARTS = 5
STEPS_DEV = REGIONS // 2
EARLY = STEPS_DEV - 2
BATCH = 6
QUARTERS = GROUPS // CHUNK

sharpness = 12.0
montage_stiffness = 1.0
section_stiffness = 1.0
anchor_stiffness = 0.05
step_length = 0.2

F32 = jnp.float32
BF16 = jnp.bfloat16
MESH = pl.DeviceIdType.MESH
EMPTY = 1 << 20


def tables():
    f32 = np.float32
    index = np.arange(WIN)
    step = f32(2.0 * math.pi / WIN)

    def rounded(fn, phase):
        angle = (phase % WIN).astype(f32) * step
        return fn(angle.astype(np.float64)).astype(f32).astype(ml_dtypes.bfloat16).astype(f32)

    phase = index[:, None] * index[None, :]
    cosine, sine = rounded(np.cos, phase), rounded(np.sin, phase)
    back = (np.arange(SHIFTS) - RADIUS)[:, None] * index[None, :]
    back_cos, back_sin = rounded(np.cos, back), rounded(np.sin, back)

    right = np.zeros((PHASES, 256, 256), f32)
    for m in range(PHASES):
        rows = slice(32 * m, 32 * m + WIN)
        right[m, rows, :HALF] = cosine[:, :HALF]
        right[m, rows, 128 : 128 + HALF] = -sine[:, :HALF]
    order = np.concatenate([np.arange(QUARTER) * PHASES + m for m in range(PHASES)])
    c, s = cosine[:, order], sine[:, order]
    left = np.concatenate([np.concatenate([c, s], 1), np.concatenate([-s, c], 1)], 0)
    back_left = np.zeros((2 * QROWS, 2 * WIN), f32)
    back_left[:SHIFTS] = np.concatenate([back_cos, -back_sin], 1)
    back_left[QROWS : QROWS + SHIFTS] = np.concatenate([back_sin, back_cos], 1)
    weight = np.full(HALF, 2.0, f32)
    weight[0] = weight[-1] = 1.0
    back_right = np.zeros((512, 128), f32)
    energy = np.zeros((256, 128), f32)
    member = np.zeros((8, 128), f32)
    for i in range(CAP):
        rows, lanes = HALF * i, TLANES * i
        back_right[rows : rows + HALF, lanes : lanes + SHIFTS] = weight[:, None] * back_cos[:, :HALF].T
        back_right[256 + rows : 256 + rows + HALF, lanes : lanes + SHIFTS] = (
            -weight[:, None] * back_sin[:, :HALF].T
        )
        energy[rows : rows + HALF, lanes : lanes + TLANES] = weight[:, None]
        member[i::CAP, lanes : lanes + SHIFTS] = 1.0
    member[2 * CAP :] = 0.0
    return [jnp.asarray(t.astype(ml_dtypes.bfloat16)) for t in (right, left, back_left, back_right, energy, member)]


def split3(x):
    high = x.astype(BF16)
    rest = x - high.astype(F32)
    middle = rest.astype(BF16)
    low = (rest - middle.astype(F32)).astype(BF16)
    return high, middle, low


def exact_dot(x, table):
    rows = x.shape[0]
    out = jnp.dot(jnp.concatenate(split3(x), axis=0), table, preferred_element_type=F32)
    return out[:rows] + out[rows : 2 * rows] + out[2 * rows :]


def lane_iota(rows=1):
    return lax.broadcasted_iota(jnp.int32, (rows, 128), 1)


SECTION_RECV = (
    ((1, 0), (1, 1), (1, 2)),
    ((0, 3), (2, 0), (2, 1)),
    ((1, 2), (1, 3), (3, 0)),
    ((2, 1), (2, 2), (2, 3)),
)


STEPS = (
    (0, 0, 2), (1, 0, 2), "y", (0, 0, 1), (2, 0, -1), (1, 0, 0), (-1, 0, 1), (1, 0, 1),
    (1, 1, -1), (2, 1, 1), (-1, 1, -1), "xz", (-1, 1, 0), (0, 1, -1), (-1, 1, 2), "x",
)
MUTUAL = STEPS.index((0, 0, 2))


def moved(me, step, sign):
    y, x, z = me // 8, me // 4 % 2, me % 4
    move = STEPS[step]
    if move == "y":
        upper = y // 2
        move = (2, 0, 2 * (1 - upper) if sign > 0 else 2 * upper)
    elif isinstance(move, str):
        move = (2 * (1 - x) if sign > 0 else 2 * x, 1, 2 if move == "xz" else 0)
    dy, dx, dz = move
    return (y + sign * dy + 4) % 4 * 8 + (x + dx) % 2 * 4 + (z + sign * dz + 4) % 4


def section_sends(section):
    return [
        (to, source, chunk)
        for to in range(SECTIONS)
        for chunk, (origin, source) in enumerate(SECTION_RECV[to])
        if origin == section
    ]


def flow_kernel(
    win_hbm, dev_ref, slot_ref,
    right_hbm, left_hbm, back_left_hbm, back_right_hbm, energy_hbm, member_hbm,
    out_ref,
    right_ref, left_ref, back_left_ref, back_right_ref, energy_ref, member_ref,
    win_ref, seg_re, seg_im, spectra, natural, outgoing, packed, from_section, from_region,
    cross, backs, squares, sums, dev_row, slot_row, ids_vmem, ids,
    from_slot, from_group, from_partner, published, ours, early, late, sections, field, fields,
    load_sem, ids_sem, sec_send, sec_recv, reg_send, reg_recv,
    field_send, field_recv, ours_send, ours_recv, early_send, early_recv, late_send, late_recv, ready,
):
    me = lax.axis_index("region")
    sec = lax.axis_index("sec")

    def neighbour(o):
        return {"region": (me + o) % REGIONS}

    width = WIN * WIN // PARTS
    load_right = pltpu.make_async_copy(right_hbm, right_ref, load_sem.at[PARTS])
    load_tables = [
        pltpu.make_async_copy(source, into, load_sem.at[PARTS + 1 + k])
        for k, (source, into) in enumerate(
            (
                (left_hbm, left_ref),
                (back_left_hbm, back_left_ref),
                (back_right_hbm, back_right_ref),
                (energy_hbm, energy_ref),
                (member_hbm, member_ref),
            )
        )
    ]

    def load_part(part):
        lanes = pl.ds(part * width, width)
        return pltpu.make_async_copy(
            win_hbm.at[0, :, lanes], win_ref.at[:, lanes], load_sem.at[part]
        )

    load_right.start()
    for part in range(PARTS):
        load_part(part).start()

    barrier = pltpu.get_barrier_semaphore()

    def greet(o, _):
        pl.semaphore_signal(barrier, inc=1, device_id=neighbour(o), device_id_type=MESH)
        return 0

    lax.fori_loop(1, REGIONS, greet, 0)
    for d in range(1, SECTIONS):
        pl.semaphore_signal(
            barrier, inc=1, device_id={"sec": (sec + d) % SECTIONS}, device_id_type=MESH
        )
    for load in load_tables:
        load.start()

    load_right.wait()
    for part in range(PARTS):
        load_part(part).wait()
        for m in range(PHASES):
            rows = [
                win_ref[:, 640 * q + 128 * m : 640 * q + 128 * m + 256]
                for q in range(8 * part, 8 * part + 8)
            ]
            seg = jnp.dot(
                jnp.concatenate(rows, axis=0), right_ref[m], preferred_element_type=F32
            )
            start = (QUARTER * m + 8 * part) * WIN_DEV
            seg_re[start : start + 8 * WIN_DEV, :] = seg[:, :128]
            seg_im[start : start + 8 * WIN_DEV, :] = seg[:, 128:]
    for load in load_tables:
        load.wait()

    wide = lane_iota(2 * WIN)

    def pack(windows):
        x0, x1, x2 = [spectra[w] for w in windows]
        x1 = pltpu.roll(x1, HALF, 1)
        x2 = pltpu.roll(x2, 2 * HALF - 128, 1)
        return jnp.concatenate(
            [jnp.where(wide < HALF, x0, x1), jnp.where(wide < 2 * HALF - 128, x1, x2)], axis=1
        )

    def section_copy(k, index):
        to, source, chunk = section_sends(k)[index]
        return pltpu.make_async_remote_copy(
            src_ref=natural.at[pl.ds(CHUNK * source, CHUNK)],
            dst_ref=from_section.at[pl.ds(CHUNK * chunk, CHUNK)],
            send_sem=sec_send.at[index],
            recv_sem=sec_recv.at[chunk],
            device_id={"sec": to},
            device_id_type=MESH,
        )

    def region_copy(step):
        to = moved(me, step, 1)
        return pltpu.make_async_remote_copy(
            src_ref=outgoing.at[step],
            dst_ref=from_region.at[step],
            send_sem=reg_send.at[step],
            recv_sem=reg_recv.at[step],
            device_id={"region": to},
            device_id_type=MESH,
        )

    def spectra_step(step, first):
        part = (2 * first + step) % (2 * QUARTERS)
        for pair in range(CAP):
            w = 2 * CAP * part + 2 * pair
            sides = [
                jnp.concatenate(
                    [seg[pl.ds(w + k, WIN, stride=WIN_DEV), :] for k in range(2)], axis=1
                ).astype(BF16)
                for seg in (seg_re, seg_im)
            ]
            spectrum = jnp.dot(
                left_ref[...], jnp.concatenate(sides, axis=0), preferred_element_type=F32
            ).astype(BF16)
            spectra[w] = spectrum[:, :128]
            spectra[w + 1] = spectrum[:, 128:]
        for k in range(2):
            w = 2 * CAP * part + CAP * k
            natural[2 * part + k] = pack([w, w + 1, w + 2])
        return first

    lane = lane_iota()
    start = jnp.where(sec == 1, 2, 0)
    for quarter in range(QUARTERS):
        lax.fori_loop(2 * quarter, 2 * quarter + 2, spectra_step, start)
        if quarter == 0:
            pl.semaphore_wait(barrier, REGIONS - 1 + SECTIONS - 1)
            for d in range(1, SECTIONS):
                pl.semaphore_signal(
                    ready, inc=1, device_id={"sec": (sec + d) % SECTIONS}, device_id_type=MESH
                )
        for k in range(SECTIONS):
            done = (quarter + (2 if k == 1 else 0)) % QUARTERS

            @pl.when(sec == k)
            def _():
                for index, (_, source, _) in enumerate(section_sends(k)):
                    if source == done:
                        section_copy(k, index).start()

        if quarter != 1:
            continue
        dev_row[...] = jnp.full((1, 128), -1, jnp.int32)
        slot_row[...] = jnp.full((1, 128), -1, jnp.int32)
        dev_row[0:1, 0:WIN_DEV] = dev_ref[...].reshape(1, WIN_DEV)
        slot_row[0:1, 0:WIN_DEV] = slot_ref[...].reshape(1, WIN_DEV)
        device, partner = dev_row[...], slot_row[...]
        code = jnp.where(me < device, lane, partner) * 64 + lane
        same = device == lax.broadcasted_iota(jnp.int32, (REGIONS, 128), 0)
        left_over = jnp.where(same, code, EMPTY)
        rank = jnp.zeros((1, 128), jnp.int32)
        listed = jnp.zeros((REGIONS, 128), jnp.int32)
        lane32 = lane_iota(REGIONS)
        for i in range(CAP):
            least = jnp.min(left_over, axis=1, keepdims=True)
            found = jnp.logical_and(same, left_over == least)
            rank += i * jnp.sum(jnp.where(found, 1, 0), axis=0, keepdims=True)
            window = jnp.where(least < EMPTY, least % 64, 0)
            listed = jnp.where(lane32 == i, window, listed)
            left_over = jnp.where(left_over > least, left_over, EMPTY)
        ids_vmem[...] = listed
        load_ids = pltpu.make_async_copy(ids_vmem, ids, ids_sem)
        load_ids.start()

    load_ids.wait()

    for step in range(STEPS_DEV):
        to = moved(me, step, 1)
        outgoing[step] = pack([ids[to, i] for i in range(CAP)])
        region_copy(step).start()

    row = lax.broadcasted_iota(jnp.int32, (128, 128), 0)
    column = lax.broadcasted_iota(jnp.int32, (128, 128), 1)
    origin = jnp.full((128, 128), -2, jnp.int32)
    for step in range(STEPS_DEV):
        origin = jnp.where(row == step, moved(me, step, -1), origin)
        if step != MUTUAL:
            origin = jnp.where(row == STEPS_DEV + step, moved(me, step, 1), origin)
    sign = jnp.where(row < STEPS_DEV, 1.0, -1.0)
    for i in range(CAP):
        chosen = jnp.logical_and(origin == device, rank == i)
        from_slot[:, 128 * i : 128 * i + 128] = jnp.where(chosen, sign, 0.0).astype(BF16)
        chosen = CAP * row + i == column
        chosen = jnp.logical_and(chosen, column < WIN_DEV)
        from_group[:, 128 * i : 128 * i + 128] = chosen.astype(F32).astype(BF16)
    from_partner[...] = (row == partner).astype(F32).astype(BF16)

    sums[...] = jnp.zeros_like(sums)
    row_shift = lax.broadcasted_iota(jnp.int32, (QROWS, 128), 0)
    shift_mask = jnp.logical_and(row_shift < SHIFTS, lane_iota(QROWS) % TLANES < SHIFTS)
    row_value = (row_shift - RADIUS).astype(F32)

    def correlate(first_ref, second_ref, u):
        energy_a = jnp.zeros((8, 256), F32)
        energy_b = jnp.zeros((8, 256), F32)
        for r in range(0, WIN, 32):
            ar = first_ref[r : r + 32, :].astype(F32)
            ai = first_ref[WIN + r : WIN + r + 32, :].astype(F32)
            br = second_ref[r : r + 32, :].astype(F32)
            bi = second_ref[WIN + r : WIN + r + 32, :].astype(F32)
            scale = 1.0 / (WIN * WIN)
            cross[u, r : r + 32, :] = ((ar * br + ai * bi) * scale).astype(BF16)
            cross[u, WIN + r : WIN + r + 32, :] = ((ai * br - ar * bi) * scale).astype(BF16)
            energy_a += jnp.sum((ar * ar + ai * ai).reshape(4, 8, 256), axis=0)
            energy_b += jnp.sum((br * br + bi * bi).reshape(4, 8, 256), axis=0)
        squares[16 * u : 16 * u + 8, :] = energy_a
        squares[16 * u + 8 : 16 * u + 16, :] = energy_b
        back = jnp.dot(back_left_ref[...], cross[u], preferred_element_type=F32).astype(BF16)
        backs[QROWS * u : QROWS * u + QROWS, :256] = back[:QROWS]
        backs[QROWS * u : QROWS * u + QROWS, 256:] = back[QROWS:]

    column_value = (lane % TLANES - RADIUS).astype(F32)
    lane8 = lane_iota(8)
    row8 = lax.broadcasted_iota(jnp.int32, (8, 128), 0)

    def weigh(count):
        surfaces = jnp.dot(
            backs[: QROWS * count], back_right_ref[...], preferred_element_type=F32
        )
        energies = exact_dot(squares[: 16 * count], energy_ref[...]) / (WIN * WIN)
        for u in range(count):
            first = jnp.sum(energies[16 * u : 16 * u + 8], axis=0, keepdims=True)
            second = jnp.sum(energies[16 * u + 8 : 16 * u + 16], axis=0, keepdims=True)
            norm = jnp.sqrt(first * second + 1e-06)
            surface = surfaces[QROWS * u : QROWS * u + QROWS]
            weights = jnp.where(shift_mask, jnp.exp(sharpness * (surface / norm)), 0.0)
            total = jnp.sum(weights, axis=0, keepdims=True)
            sums[u : u + 1, :] = total
            sums[8 + u : 9 + u, :] = jnp.sum(weights * row_value, axis=0, keepdims=True)
            sums[16 + u : 17 + u, :] = total * column_value
        parts = [
            lax.dot_general(
                member_ref[...], part, (((1,), (1,)), ((), ())), preferred_element_type=F32
            )
            for part in split3(sums[...])
        ]
        total = parts[0] + parts[1] + parts[2]
        moment = jnp.where(row8 < CAP, pltpu.roll(total, 128 - 8, 1), pltpu.roll(total, 128 - 16, 1))
        flows = moment / jnp.where(total == 0.0, 1.0, total)
        return jnp.where(jnp.logical_and(jnp.abs(flows) <= 2.0 * RADIUS, lane8 < count), flows, 0.0)

    def section_batch(chunk, _):
        pltpu.make_async_remote_copy(
            src_ref=natural.at[pl.ds(0, CHUNK)],
            dst_ref=from_section.at[pl.ds(CHUNK * chunk, CHUNK)],
            send_sem=sec_send.at[0],
            recv_sem=sec_recv.at[chunk],
            device_id={"sec": (sec + 1) % SECTIONS},
            device_id_type=MESH,
        ).wait_recv()
        first = CHUNK * ((SHARE // CHUNK * sec + chunk) % QUARTERS)
        for u in range(CHUNK):
            correlate(natural.at[first + u], from_section.at[CHUNK * chunk + u], u)
        flows = weigh(CHUNK)
        flows = jnp.where(chunk < sec, -flows, flows)
        sections[...] += pltpu.roll(flows, CHUNK * chunk, 1)
        return 0

    def early_copy(step):
        return pltpu.make_async_remote_copy(
            src_ref=published.at[0],
            dst_ref=early.at[step],
            send_sem=early_send,
            recv_sem=early_recv,
            device_id={"region": moved(me, step, -1)},
            device_id_type=MESH,
        )

    def late_copy(step, k):
        return pltpu.make_async_remote_copy(
            src_ref=published.at[1],
            dst_ref=late.at[step - EARLY, sec],
            send_sem=late_send,
            recv_sem=late_recv,
            device_id={"sec": k, "region": moved(me, step, -1)},
            device_id_type=MESH,
        )

    def ours_copy(d):
        return pltpu.make_async_remote_copy(
            src_ref=ours.at[0],
            dst_ref=ours.at[d],
            send_sem=ours_send,
            recv_sem=ours_recv,
            device_id={"sec": (sec + d) % SECTIONS},
            device_id_type=MESH,
        )

    def field_copy(o):
        return pltpu.make_async_remote_copy(
            src_ref=field,
            dst_ref=fields.at[REGIONS - 1 - o],
            send_sem=field_send,
            recv_sem=field_recv,
            device_id=neighbour(o),
            device_id_type=MESH,
        )

    def region_batch(first, last):
        for u, step in enumerate(range(first, last)):
            origin = moved(me, step, -1)
            packed[u] = pack([ids[origin, i] for i in range(CAP)])
            region_copy(step).wait_recv()
            correlate(packed.at[u], from_region.at[step], u)
        flows = weigh(last - first)
        flows += pltpu.roll(flows, STEPS_DEV, 1)
        return pltpu.roll(flows, first, 1) if first else flows

    def by_window(x, table):
        spread = exact_dot(x, table)
        rows = []
        for k in range(x.shape[0] // 8):
            for c in range(2):
                at = 8 * k + CAP * c
                rows.append(
                    sum(spread[at + i : at + i + 1, 128 * i : 128 * i + 128] for i in range(CAP))
                )
        return rows

    sections[...] = jnp.zeros((8, 128), F32)
    chunks = SHARE // CHUNK
    low = jnp.where(sec == 2, chunks - 1, 0)
    high = jnp.where(sec == 1, 1, chunks)
    lax.fori_loop(low, high, section_batch, 0)
    flows = region_batch(0, 4)
    lax.fori_loop(0, low, section_batch, 0)
    lax.fori_loop(high, chunks, section_batch, 0)
    section = sections[...]
    shift = section
    for k in range(1, SECTIONS):
        shift = jnp.where(sec == k, pltpu.roll(section, SHARE * k, 1), shift)
    edges = [shift] + [pltpu.roll(shift, 128 - GROUPS * e, 1) for e in range(1, SECTIONS - 1)]
    edges = [jnp.where(lane8 < GROUPS, edge, 0.0) for edge in edges]
    section_rows = by_window(jnp.concatenate(edges, axis=0), from_group[...])
    section = jnp.concatenate(section_rows + [jnp.zeros((2, 128), F32)], axis=0)
    field[...] = section

    def field_start(o, _):
        field_copy(o).start()
        return 0

    lax.fori_loop(1, REGIONS, field_start, 0)
    pl.semaphore_wait(ready, SECTIONS - 1)
    flows += region_batch(4, 8)
    flows += region_batch(8, EARLY)
    published[0] = flows
    for step in range(EARLY):
        early_copy(step).start()
    flows += region_batch(EARLY, STEPS_DEV)
    published[1] = flows
    for step in range(EARLY, STEPS_DEV):
        for k in range(SECTIONS):
            late_copy(step, k).start()

    pltpu.make_async_copy(fields, fields, field_recv).wait()
    found = exact_dot(fields[...].reshape(8 * (REGIONS - 1), 128), from_partner[...])
    partner_section = jnp.zeros((8, 128), F32)
    for o in range(1, REGIONS):
        here = jnp.broadcast_to(device, (8, 128)) == (me + o) % REGIONS
        partner_section = jnp.where(here, found[8 * o - 8 : 8 * o], partner_section)
    pltpu.make_async_copy(early, early, early_recv).wait()
    for step in range(EARLY):
        flows = jnp.where(lane8 == STEPS_DEV + step, early[step], flows)
    ours[0, 0:8, :] = flows
    ours[0, 8:16, :] = section
    ours[0, 16:24, :] = partner_section
    for d in range(1, SECTIONS):
        ours_copy(d).start()
    for k in range(SECTIONS):

        @pl.when(sec == k)
        def _():
            for index in range(len(section_sends(k))):
                section_copy(k, index).wait_send()

    for step in range(STEPS_DEV):
        region_copy(step).wait_send()
    pltpu.make_async_copy(fields, fields, field_send).wait()
    pltpu.make_async_copy(early, early, early_send).wait()
    pltpu.make_async_copy(late, late, late_recv).wait()
    others = ours.at[pl.ds(1, SECTIONS - 1)]
    pltpu.make_async_copy(others, others, ours_recv).wait()
    blocks = []
    for k in range(SECTIONS):
        block = ours[(sec - k + SECTIONS) % SECTIONS, 0:8, :]
        for step in range(EARLY, STEPS_DEV):
            block = jnp.where(lane8 == STEPS_DEV + step, late[step - EARLY, k], block)
        blocks.append(block)
    montage = jnp.concatenate(
        by_window(jnp.concatenate(blocks, axis=0), from_slot[...]), axis=0
    )
    section = ours[0, 8:16, :] + ours[1, 8:16, :] + ours[2, 8:16, :] + ours[3, 8:16, :]
    partner_section = ours[0, 16:24, :] + ours[1, 16:24, :] + ours[2, 16:24, :] + ours[3, 16:24, :]

    has_next = jnp.where(row8 < 2 * (SECTIONS - 1), 1.0, 0.0)
    has_prev = jnp.where(row8 >= 2, 1.0, 0.0)
    disagreement = 2.0 * montage

    def before(x):
        return pltpu.roll(x, 2, 0)

    def after(x):
        return pltpu.roll(x, 6, 0)

    def relax(u, p, apart, flow, previous):
        gradient = (
            montage_stiffness * (2.0 * u - 2.0 * p - apart)
            + section_stiffness * has_next * (u - after(u) - flow)
            - section_stiffness * has_prev * (before(u) - u - previous)
            + anchor_stiffness * u
        )
        return u - step_length * gradient

    previous, partner_previous = before(section), before(partner_section)

    def turn(_, state):
        u, p = state
        return (
            relax(u, p, disagreement, section, previous),
            relax(p, u, -disagreement, partner_section, partner_previous),
        )

    zero = jnp.zeros((8, 128), F32)
    shift, _ = lax.fori_loop(0, ITERS, turn, (zero, zero))
    for k, values in enumerate((montage, section, shift)):
        chosen = values[0:2]
        for n in range(1, SECTIONS):
            chosen = jnp.where(sec == n, values[2 * n : 2 * n + 2], chosen)
        out_ref[2 * k : 2 * k + 2, :] = chosen
    out_ref[6:8, :] = jnp.zeros((2, 128), F32)

    pltpu.make_async_copy(late, late, late_send).wait()
    pltpu.make_async_copy(others, others, ours_send).wait()


def split_kernel(rows_ref, montage_ref, section_ref, shift_ref):
    for k, ref in enumerate((montage_ref, section_ref, shift_ref)):
        ref[0] = rows_ref[2 * k : 2 * k + 2, :WIN_DEV]


VMEM = pl.BlockSpec(memory_space=pltpu.VMEM)
ANY = pl.BlockSpec(memory_space=pl.ANY)


def body(windows, partner_dev, partner_slot):
    side = (2 * WIN, 256)
    dma = pltpu.SemaphoreType.DMA
    rows = pl.pallas_call(
        flow_kernel,
        out_shape=jax.ShapeDtypeStruct((8, 128), F32),
        in_specs=[ANY, VMEM, VMEM] + [ANY] * 6,
        out_specs=VMEM,
        scratch_shapes=[
            pltpu.VMEM((PHASES, 256, 256), BF16),
            pltpu.VMEM((2 * WIN, 2 * WIN), BF16),
            pltpu.VMEM((2 * QROWS, 2 * WIN), BF16),
            pltpu.VMEM((512, 128), BF16),
            pltpu.VMEM((256, 128), BF16),
            pltpu.VMEM((8, 128), BF16),
            pltpu.VMEM((WIN_DEV, WIN * WIN), BF16),
            pltpu.VMEM((WIN * WIN_DEV, 128), F32),
            pltpu.VMEM((WIN * WIN_DEV, 128), F32),
            pltpu.VMEM((WIN_DEV, 2 * WIN, 128), BF16),
            pltpu.VMEM((GROUPS,) + side, BF16),
            pltpu.VMEM((STEPS_DEV,) + side, BF16),
            pltpu.VMEM((BATCH,) + side, BF16),
            pltpu.VMEM((SHARE,) + side, BF16),
            pltpu.VMEM((STEPS_DEV,) + side, BF16),
            pltpu.VMEM((BATCH,) + side, BF16),
            pltpu.VMEM((BATCH * QROWS, 512), BF16),
            pltpu.VMEM((BATCH * 16, 256), F32),
            pltpu.VMEM((128, 128), F32),
            pltpu.VMEM((1, 128), jnp.int32),
            pltpu.VMEM((1, 128), jnp.int32),
            pltpu.VMEM((REGIONS, 128), jnp.int32),
            pltpu.SMEM((REGIONS, 128), jnp.int32),
            pltpu.VMEM((128, CAP * 128), BF16),
            pltpu.VMEM((128, CAP * 128), BF16),
            pltpu.VMEM((128, 128), BF16),
            pltpu.VMEM((2, 8, 128), F32),
            pltpu.VMEM((SECTIONS, 24, 128), F32),
            pltpu.VMEM((EARLY, 8, 128), F32),
            pltpu.VMEM((STEPS_DEV - EARLY, SECTIONS, 8, 128), F32),
            pltpu.VMEM((8, 128), F32),
            pltpu.VMEM((8, 128), F32),
            pltpu.VMEM((REGIONS - 1, 8, 128), F32),
            dma((PARTS + 6,)),
            dma,
            dma((5,)),
            dma((SHARE // CHUNK,)),
            dma((STEPS_DEV,)),
            dma((STEPS_DEV,)),
            dma,
            dma,
            dma,
            dma,
            dma,
            dma,
            dma,
            dma,
            pltpu.SemaphoreType.REGULAR,
        ],
        compiler_params=pltpu.CompilerParams(
            vmem_limit_bytes=60 << 20, collective_id=0, has_side_effects=True
        ),
        name="flows",
    )(windows, partner_dev, partner_slot, *tables())
    out = jax.ShapeDtypeStruct((1, 2, WIN_DEV), F32)
    return pl.pallas_call(
        split_kernel,
        out_shape=(out, out, out),
        in_specs=[VMEM],
        out_specs=(VMEM, VMEM, VMEM),
        name="split",
    )(rows)


def solution(mesh):
    placed = (P("sec", "region", None), P("region"), P("region"))
    return jax.shard_map(
        body,
        mesh=mesh,
        in_specs=placed,
        out_specs=(P("sec", None, "region"),) * 3,
        check_vma=False,
    )
```

```python
import functools
import math

import jax
import jax.numpy as jnp
import ml_dtypes
import numpy as np
from jax import lax
from jax.experimental import pallas as pl
from jax.experimental.pallas import tpu as pltpu
from jax.sharding import PartitionSpec as P

WIN = 160
RADIUS = 16
SHIFTS = 33
ITERS = 32
HALF = WIN // 2 + 1
CAP = 3
REGIONS = 32
SECTIONS = 4
WIN_DEV = 48
GROUPS = WIN_DEV // CAP
SHARE = 12
CHUNK = 4
QROWS = 48
TLANES = 40
PHASES = 4
QUARTER = WIN // PHASES
PARTS = 5
STEPS_DEV = REGIONS // 2
EARLY = STEPS_DEV - 2
BATCH = 6
QUARTERS = GROUPS // CHUNK

sharpness = 12.0
montage_stiffness = 1.0
section_stiffness = 1.0
anchor_stiffness = 0.05
step_length = 0.2

F32 = jnp.float32
BF16 = jnp.bfloat16
MESH = pl.DeviceIdType.MESH
EMPTY = 1 << 20


def tables():
    f32 = np.float32
    index = np.arange(WIN)
    step = f32(2.0 * math.pi / WIN)

    def rounded(fn, phase):
        angle = (phase % WIN).astype(f32) * step
        return fn(angle.astype(np.float64)).astype(f32).astype(ml_dtypes.bfloat16).astype(f32)

    phase = index[:, None] * index[None, :]
    cosine, sine = rounded(np.cos, phase), rounded(np.sin, phase)
    back = (np.arange(SHIFTS) - RADIUS)[:, None] * index[None, :]
    back_cos, back_sin = rounded(np.cos, back), rounded(np.sin, back)

    right = np.zeros((PHASES, 256, 256), f32)
    for m in range(PHASES):
        rows = slice(32 * m, 32 * m + WIN)
        right[m, rows, :HALF] = cosine[:, :HALF]
        right[m, rows, 128 : 128 + HALF] = -sine[:, :HALF]
    order = np.concatenate([np.arange(QUARTER) * PHASES + m for m in range(PHASES)])
    c, s = cosine[:, order], sine[:, order]
    left = np.concatenate([np.concatenate([c, s], 1), np.concatenate([-s, c], 1)], 0)
    back_left = np.zeros((2 * QROWS, 2 * WIN), f32)
    back_left[:SHIFTS] = np.concatenate([back_cos, -back_sin], 1)
    back_left[QROWS : QROWS + SHIFTS] = np.concatenate([back_sin, back_cos], 1)
    weight = np.full(HALF, 2.0, f32)
    weight[0] = weight[-1] = 1.0
    back_right = np.zeros((512, 128), f32)
    energy = np.zeros((256, 128), f32)
    member = np.zeros((8, 128), f32)
    for i in range(CAP):
        rows, lanes = HALF * i, TLANES * i
        back_right[rows : rows + HALF, lanes : lanes + SHIFTS] = weight[:, None] * back_cos[:, :HALF].T
        back_right[256 + rows : 256 + rows + HALF, lanes : lanes + SHIFTS] = (
            -weight[:, None] * back_sin[:, :HALF].T
        )
        energy[rows : rows + HALF, lanes : lanes + TLANES] = weight[:, None]
        member[i::CAP, lanes : lanes + SHIFTS] = 1.0
    member[2 * CAP :] = 0.0
    return [jnp.asarray(t.astype(ml_dtypes.bfloat16)) for t in (right, left, back_left, back_right, energy, member)]


def split3(x):
    high = x.astype(BF16)
    rest = x - high.astype(F32)
    middle = rest.astype(BF16)
    low = (rest - middle.astype(F32)).astype(BF16)
    return high, middle, low


def exact_dot(x, table):
    rows = x.shape[0]
    out = jnp.dot(jnp.concatenate(split3(x), axis=0), table, preferred_element_type=F32)
    return out[:rows] + out[rows : 2 * rows] + out[2 * rows :]


def lane_iota(rows=1):
    return lax.broadcasted_iota(jnp.int32, (rows, 128), 1)


SECTION_RECV = (
    ((1, 0), (1, 1), (1, 2)),
    ((0, 3), (2, 0), (2, 1)),
    ((1, 2), (1, 3), (3, 0)),
    ((2, 1), (2, 2), (2, 3)),
)


STEPS = (
    (0, 0, 2), (1, 0, 2), "y", (0, 0, 1), (2, 0, -1), (1, 0, 0), (-1, 0, 1), (1, 0, 1),
    (1, 1, -1), (2, 1, 1), (-1, 1, -1), "xz", (-1, 1, 0), (0, 1, -1), (-1, 1, 2), "x",
)
MUTUAL = STEPS.index((0, 0, 2))


def moved(me, step, sign):
    y, x, z = me // 8, me // 4 % 2, me % 4
    move = STEPS[step]
    if move == "y":
        upper = y // 2
        move = (2, 0, 2 * (1 - upper) if sign > 0 else 2 * upper)
    elif isinstance(move, str):
        move = (2 * (1 - x) if sign > 0 else 2 * x, 1, 2 if move == "xz" else 0)
    dy, dx, dz = move
    return (y + sign * dy + 4) % 4 * 8 + (x + dx) % 2 * 4 + (z + sign * dz + 4) % 4


def section_sends(section):
    return [
        (to, source, chunk)
        for to in range(SECTIONS)
        for chunk, (origin, source) in enumerate(SECTION_RECV[to])
        if origin == section
    ]


def flow_kernel(
    win_hbm, dev_ref, slot_ref,
    right_hbm, left_hbm, back_left_hbm, back_right_hbm, energy_hbm, member_hbm,
    out_ref,
    right_ref, left_ref, back_left_ref, back_right_ref, energy_ref, member_ref,
    win_ref, seg_re, seg_im, spectra, natural, outgoing, packed, from_section, from_region,
    cross, backs, squares, sums, dev_row, slot_row, ids_vmem, ids,
    from_slot, from_group, from_partner, published, ours, early, late, sections, field, fields,
    load_sem, ids_sem, sec_send, sec_recv, reg_send, reg_recv,
    field_send, field_recv, ours_send, ours_recv, early_send, early_recv, late_send, late_recv, ready,
):
    me = lax.axis_index("region")
    sec = lax.axis_index("sec")

    def neighbour(o):
        return {"region": (me + o) % REGIONS}

    width = WIN * WIN // PARTS
    load_right = pltpu.make_async_copy(right_hbm, right_ref, load_sem.at[PARTS])
    load_tables = [
        pltpu.make_async_copy(source, into, load_sem.at[PARTS + 1 + k])
        for k, (source, into) in enumerate(
            (
                (left_hbm, left_ref),
                (back_left_hbm, back_left_ref),
                (back_right_hbm, back_right_ref),
                (energy_hbm, energy_ref),
                (member_hbm, member_ref),
            )
        )
    ]

    def load_part(part):
        lanes = pl.ds(part * width, width)
        return pltpu.make_async_copy(
            win_hbm.at[0, :, lanes], win_ref.at[:, lanes], load_sem.at[part]
        )

    load_right.start()
    for part in range(PARTS):
        load_part(part).start()

    barrier = pltpu.get_barrier_semaphore()

    def greet(o, _):
        pl.semaphore_signal(barrier, inc=1, device_id=neighbour(o), device_id_type=MESH)
        return 0

    lax.fori_loop(1, REGIONS, greet, 0)
    for d in range(1, SECTIONS):
        pl.semaphore_signal(
            barrier, inc=1, device_id={"sec": (sec + d) % SECTIONS}, device_id_type=MESH
        )
    for load in load_tables:
        load.start()

    load_right.wait()
    for part in range(PARTS):
        load_part(part).wait()
        for m in range(PHASES):
            rows = [
                win_ref[:, 640 * q + 128 * m : 640 * q + 128 * m + 256]
                for q in range(8 * part, 8 * part + 8)
            ]
            seg = jnp.dot(
                jnp.concatenate(rows, axis=0), right_ref[m], preferred_element_type=F32
            )
            start = (QUARTER * m + 8 * part) * WIN_DEV
            seg_re[start : start + 8 * WIN_DEV, :] = seg[:, :128]
            seg_im[start : start + 8 * WIN_DEV, :] = seg[:, 128:]
    for load in load_tables:
        load.wait()

    wide = lane_iota(2 * WIN)

    def pack(windows):
        x0, x1, x2 = [spectra[w] for w in windows]
        x1 = pltpu.roll(x1, HALF, 1)
        x2 = pltpu.roll(x2, 2 * HALF - 128, 1)
        return jnp.concatenate(
            [jnp.where(wide < HALF, x0, x1), jnp.where(wide < 2 * HALF - 128, x1, x2)], axis=1
        )

    def section_copy(k, index):
        to, source, chunk = section_sends(k)[index]
        return pltpu.make_async_remote_copy(
            src_ref=natural.at[pl.ds(CHUNK * source, CHUNK)],
            dst_ref=from_section.at[pl.ds(CHUNK * chunk, CHUNK)],
            send_sem=sec_send.at[index],
            recv_sem=sec_recv.at[chunk],
            device_id={"sec": to},
            device_id_type=MESH,
        )

    def region_copy(step):
        to = moved(me, step, 1)
        return pltpu.make_async_remote_copy(
            src_ref=outgoing.at[step],
            dst_ref=from_region.at[step],
            send_sem=reg_send.at[step],
            recv_sem=reg_recv.at[step],
            device_id={"region": to},
            device_id_type=MESH,
        )

    def spectra_step(step, first):
        part = (2 * first + step) % (2 * QUARTERS)
        for pair in range(CAP):
            w = 2 * CAP * part + 2 * pair
            sides = [
                jnp.concatenate(
                    [seg[pl.ds(w + k, WIN, stride=WIN_DEV), :] for k in range(2)], axis=1
                ).astype(BF16)
                for seg in (seg_re, seg_im)
            ]
            spectrum = jnp.dot(
                left_ref[...], jnp.concatenate(sides, axis=0), preferred_element_type=F32
            ).astype(BF16)
            spectra[w] = spectrum[:, :128]
            spectra[w + 1] = spectrum[:, 128:]
        for k in range(2):
            w = 2 * CAP * part + CAP * k
            natural[2 * part + k] = pack([w, w + 1, w + 2])
        return first

    lane = lane_iota()
    start = jnp.where(sec == 1, 2, 0)
    for quarter in range(QUARTERS):
        lax.fori_loop(2 * quarter, 2 * quarter + 2, spectra_step, start)
        if quarter == 0:
            pl.semaphore_wait(barrier, REGIONS - 1 + SECTIONS - 1)
            for d in range(1, SECTIONS):
                pl.semaphore_signal(
                    ready, inc=1, device_id={"sec": (sec + d) % SECTIONS}, device_id_type=MESH
                )
        for k in range(SECTIONS):
            done = (quarter + (2 if k == 1 else 0)) % QUARTERS

            @pl.when(sec == k)
            def _():
                for index, (_, source, _) in enumerate(section_sends(k)):
                    if source == done:
                        section_copy(k, index).start()

        if quarter != 1:
            continue
        dev_row[...] = jnp.full((1, 128), -1, jnp.int32)
        slot_row[...] = jnp.full((1, 128), -1, jnp.int32)
        dev_row[0:1, 0:WIN_DEV] = dev_ref[...].reshape(1, WIN_DEV)
        slot_row[0:1, 0:WIN_DEV] = slot_ref[...].reshape(1, WIN_DEV)
        device, partner = dev_row[...], slot_row[...]
        code = jnp.where(me < device, lane, partner) * 64 + lane
        same = device == lax.broadcasted_iota(jnp.int32, (REGIONS, 128), 0)
        left_over = jnp.where(same, code, EMPTY)
        rank = jnp.zeros((1, 128), jnp.int32)
        listed = jnp.zeros((REGIONS, 128), jnp.int32)
        lane32 = lane_iota(REGIONS)
        for i in range(CAP):
            least = jnp.min(left_over, axis=1, keepdims=True)
            found = jnp.logical_and(same, left_over == least)
            rank += i * jnp.sum(jnp.where(found, 1, 0), axis=0, keepdims=True)
            window = jnp.where(least < EMPTY, least % 64, 0)
            listed = jnp.where(lane32 == i, window, listed)
            left_over = jnp.where(left_over > least, left_over, EMPTY)
        ids_vmem[...] = listed
        load_ids = pltpu.make_async_copy(ids_vmem, ids, ids_sem)
        load_ids.start()

    load_ids.wait()

    across = STEPS_DEV // 2
    for step in [n + k for n in range(across) for k in (across, 0)]:
        to = moved(me, step, 1)
        outgoing[step] = pack([ids[to, i] for i in range(CAP)])
        region_copy(step).start()

    row = lax.broadcasted_iota(jnp.int32, (128, 128), 0)
    column = lax.broadcasted_iota(jnp.int32, (128, 128), 1)
    origin = jnp.full((128, 128), -2, jnp.int32)
    for step in range(STEPS_DEV):
        origin = jnp.where(row == step, moved(me, step, -1), origin)
        if step != MUTUAL:
            origin = jnp.where(row == STEPS_DEV + step, moved(me, step, 1), origin)
    sign = jnp.where(row < STEPS_DEV, 1.0, -1.0)
    for i in range(CAP):
        chosen = jnp.logical_and(origin == device, rank == i)
        from_slot[:, 128 * i : 128 * i + 128] = jnp.where(chosen, sign, 0.0).astype(BF16)
        chosen = CAP * row + i == column
        chosen = jnp.logical_and(chosen, column < WIN_DEV)
        from_group[:, 128 * i : 128 * i + 128] = chosen.astype(F32).astype(BF16)
    from_partner[...] = (row == partner).astype(F32).astype(BF16)

    sums[...] = jnp.zeros_like(sums)
    row_shift = lax.broadcasted_iota(jnp.int32, (QROWS, 128), 0)
    shift_mask = jnp.logical_and(row_shift < SHIFTS, lane_iota(QROWS) % TLANES < SHIFTS)
    row_value = (row_shift - RADIUS).astype(F32)

    def correlate(first_ref, second_ref, u):
        energy_a = jnp.zeros((8, 256), F32)
        energy_b = jnp.zeros((8, 256), F32)
        for r in range(0, WIN, 32):
            ar = first_ref[r : r + 32, :].astype(F32)
            ai = first_ref[WIN + r : WIN + r + 32, :].astype(F32)
            br = second_ref[r : r + 32, :].astype(F32)
            bi = second_ref[WIN + r : WIN + r + 32, :].astype(F32)
            scale = 1.0 / (WIN * WIN)
            cross[u, r : r + 32, :] = ((ar * br + ai * bi) * scale).astype(BF16)
            cross[u, WIN + r : WIN + r + 32, :] = ((ai * br - ar * bi) * scale).astype(BF16)
            energy_a += jnp.sum((ar * ar + ai * ai).reshape(4, 8, 256), axis=0)
            energy_b += jnp.sum((br * br + bi * bi).reshape(4, 8, 256), axis=0)
        squares[16 * u : 16 * u + 8, :] = energy_a
        squares[16 * u + 8 : 16 * u + 16, :] = energy_b
        back = jnp.dot(back_left_ref[...], cross[u], preferred_element_type=F32).astype(BF16)
        backs[QROWS * u : QROWS * u + QROWS, :256] = back[:QROWS]
        backs[QROWS * u : QROWS * u + QROWS, 256:] = back[QROWS:]

    column_value = (lane % TLANES - RADIUS).astype(F32)
    lane8 = lane_iota(8)
    row8 = lax.broadcasted_iota(jnp.int32, (8, 128), 0)

    def weigh(count):
        surfaces = jnp.dot(
            backs[: QROWS * count], back_right_ref[...], preferred_element_type=F32
        )
        energies = exact_dot(squares[: 16 * count], energy_ref[...]) / (WIN * WIN)
        for u in range(count):
            first = jnp.sum(energies[16 * u : 16 * u + 8], axis=0, keepdims=True)
            second = jnp.sum(energies[16 * u + 8 : 16 * u + 16], axis=0, keepdims=True)
            norm = jnp.sqrt(first * second + 1e-06)
            surface = surfaces[QROWS * u : QROWS * u + QROWS]
            weights = jnp.where(shift_mask, jnp.exp(sharpness * (surface / norm)), 0.0)
            total = jnp.sum(weights, axis=0, keepdims=True)
            sums[u : u + 1, :] = total
            sums[8 + u : 9 + u, :] = jnp.sum(weights * row_value, axis=0, keepdims=True)
            sums[16 + u : 17 + u, :] = total * column_value
        parts = [
            lax.dot_general(
                member_ref[...], part, (((1,), (1,)), ((), ())), preferred_element_type=F32
            )
            for part in split3(sums[...])
        ]
        total = parts[0] + parts[1] + parts[2]
        moment = jnp.where(row8 < CAP, pltpu.roll(total, 128 - 8, 1), pltpu.roll(total, 128 - 16, 1))
        flows = moment / jnp.where(total == 0.0, 1.0, total)
        return jnp.where(jnp.logical_and(jnp.abs(flows) <= 2.0 * RADIUS, lane8 < count), flows, 0.0)

    def section_batch(chunk, _):
        pltpu.make_async_remote_copy(
            src_ref=natural.at[pl.ds(0, CHUNK)],
            dst_ref=from_section.at[pl.ds(CHUNK * chunk, CHUNK)],
            send_sem=sec_send.at[0],
            recv_sem=sec_recv.at[chunk],
            device_id={"sec": (sec + 1) % SECTIONS},
            device_id_type=MESH,
        ).wait_recv()
        first = CHUNK * ((SHARE // CHUNK * sec + chunk) % QUARTERS)
        for u in range(CHUNK):
            correlate(natural.at[first + u], from_section.at[CHUNK * chunk + u], u)
        flows = weigh(CHUNK)
        flows = jnp.where(chunk < sec, -flows, flows)
        sections[...] += pltpu.roll(flows, CHUNK * chunk, 1)
        return 0

    def early_copy(step):
        return pltpu.make_async_remote_copy(
            src_ref=published.at[0],
            dst_ref=early.at[step],
            send_sem=early_send,
            recv_sem=early_recv,
            device_id={"region": moved(me, step, -1)},
            device_id_type=MESH,
        )

    def late_copy(step, k):
        return pltpu.make_async_remote_copy(
            src_ref=published.at[1],
            dst_ref=late.at[step - EARLY, sec],
            send_sem=late_send,
            recv_sem=late_recv,
            device_id={"sec": k, "region": moved(me, step, -1)},
            device_id_type=MESH,
        )

    def ours_copy(d):
        return pltpu.make_async_remote_copy(
            src_ref=ours.at[0],
            dst_ref=ours.at[d],
            send_sem=ours_send,
            recv_sem=ours_recv,
            device_id={"sec": (sec + d) % SECTIONS},
            device_id_type=MESH,
        )

    def field_copy(o):
        return pltpu.make_async_remote_copy(
            src_ref=field,
            dst_ref=fields.at[REGIONS - 1 - o],
            send_sem=field_send,
            recv_sem=field_recv,
            device_id=neighbour(o),
            device_id_type=MESH,
        )

    def region_batch(first, last):
        for u, step in enumerate(range(first, last)):
            origin = moved(me, step, -1)
            packed[u] = pack([ids[origin, i] for i in range(CAP)])
            region_copy(step).wait_recv()
            correlate(packed.at[u], from_region.at[step], u)
        flows = weigh(last - first)
        flows += pltpu.roll(flows, STEPS_DEV, 1)
        return pltpu.roll(flows, first, 1) if first else flows

    def by_window(x, table):
        spread = exact_dot(x, table)
        rows = []
        for k in range(x.shape[0] // 8):
            for c in range(2):
                at = 8 * k + CAP * c
                rows.append(
                    sum(spread[at + i : at + i + 1, 128 * i : 128 * i + 128] for i in range(CAP))
                )
        return rows

    sections[...] = jnp.zeros((8, 128), F32)
    chunks = SHARE // CHUNK
    low = jnp.where(sec == 2, chunks - 1, 0)
    high = jnp.where(sec == 1, 1, chunks)
    lax.fori_loop(low, high, section_batch, 0)
    flows = region_batch(0, 4)
    lax.fori_loop(0, low, section_batch, 0)
    lax.fori_loop(high, chunks, section_batch, 0)
    section = sections[...]
    shift = section
    for k in range(1, SECTIONS):
        shift = jnp.where(sec == k, pltpu.roll(section, SHARE * k, 1), shift)
    edges = [shift] + [pltpu.roll(shift, 128 - GROUPS * e, 1) for e in range(1, SECTIONS - 1)]
    edges = [jnp.where(lane8 < GROUPS, edge, 0.0) for edge in edges]
    section_rows = by_window(jnp.concatenate(edges, axis=0), from_group[...])
    section = jnp.concatenate(section_rows + [jnp.zeros((2, 128), F32)], axis=0)
    field[...] = section

    def field_start(o, _):
        field_copy(o).start()
        return 0

    lax.fori_loop(1, REGIONS, field_start, 0)
    pl.semaphore_wait(ready, SECTIONS - 1)
    flows += region_batch(4, 8)
    flows += region_batch(8, EARLY)
    published[0] = flows
    for step in range(EARLY):
        early_copy(step).start()
    flows += region_batch(EARLY, STEPS_DEV)
    published[1] = flows
    for step in range(EARLY, STEPS_DEV):
        for k in range(SECTIONS):
            late_copy(step, k).start()

    pltpu.make_async_copy(fields, fields, field_recv).wait()
    found = exact_dot(fields[...].reshape(8 * (REGIONS - 1), 128), from_partner[...])
    partner_section = jnp.zeros((8, 128), F32)
    for o in range(1, REGIONS):
        here = jnp.broadcast_to(device, (8, 128)) == (me + o) % REGIONS
        partner_section = jnp.where(here, found[8 * o - 8 : 8 * o], partner_section)
    pltpu.make_async_copy(early, early, early_recv).wait()
    for step in range(EARLY):
        flows = jnp.where(lane8 == STEPS_DEV + step, early[step], flows)
    ours[0, 0:8, :] = flows
    ours[0, 8:16, :] = section
    ours[0, 16:24, :] = partner_section
    for d in range(1, SECTIONS):
        ours_copy(d).start()
    for k in range(SECTIONS):

        @pl.when(sec == k)
        def _():
            for index in range(len(section_sends(k))):
                section_copy(k, index).wait_send()

    for step in range(STEPS_DEV):
        region_copy(step).wait_send()
    pltpu.make_async_copy(fields, fields, field_send).wait()
    pltpu.make_async_copy(early, early, early_send).wait()
    pltpu.make_async_copy(late, late, late_recv).wait()
    others = ours.at[pl.ds(1, SECTIONS - 1)]
    pltpu.make_async_copy(others, others, ours_recv).wait()
    blocks = []
    for k in range(SECTIONS):
        block = ours[(sec - k + SECTIONS) % SECTIONS, 0:8, :]
        for step in range(EARLY, STEPS_DEV):
            block = jnp.where(lane8 == STEPS_DEV + step, late[step - EARLY, k], block)
        blocks.append(block)
    montage = jnp.concatenate(
        by_window(jnp.concatenate(blocks, axis=0), from_slot[...]), axis=0
    )
    section = ours[0, 8:16, :] + ours[1, 8:16, :] + ours[2, 8:16, :] + ours[3, 8:16, :]
    partner_section = ours[0, 16:24, :] + ours[1, 16:24, :] + ours[2, 16:24, :] + ours[3, 16:24, :]

    has_next = jnp.where(row8 < 2 * (SECTIONS - 1), 1.0, 0.0)
    has_prev = jnp.where(row8 >= 2, 1.0, 0.0)
    disagreement = 2.0 * montage

    def before(x):
        return pltpu.roll(x, 2, 0)

    def after(x):
        return pltpu.roll(x, 6, 0)

    def relax(u, p, apart, flow, previous):
        gradient = (
            montage_stiffness * (2.0 * u - 2.0 * p - apart)
            + section_stiffness * has_next * (u - after(u) - flow)
            - section_stiffness * has_prev * (before(u) - u - previous)
            + anchor_stiffness * u
        )
        return u - step_length * gradient

    previous, partner_previous = before(section), before(partner_section)

    def turn(_, state):
        u, p = state
        return (
            relax(u, p, disagreement, section, previous),
            relax(p, u, -disagreement, partner_section, partner_previous),
        )

    zero = jnp.zeros((8, 128), F32)
    shift, _ = lax.fori_loop(0, ITERS, turn, (zero, zero))
    for k, values in enumerate((montage, section, shift)):
        chosen = values[0:2]
        for n in range(1, SECTIONS):
            chosen = jnp.where(sec == n, values[2 * n : 2 * n + 2], chosen)
        out_ref[2 * k : 2 * k + 2, :] = chosen
    out_ref[6:8, :] = jnp.zeros((2, 128), F32)

    pltpu.make_async_copy(late, late, late_send).wait()
    pltpu.make_async_copy(others, others, ours_send).wait()


def split_kernel(rows_ref, montage_ref, section_ref, shift_ref):
    for k, ref in enumerate((montage_ref, section_ref, shift_ref)):
        ref[0] = rows_ref[2 * k : 2 * k + 2, :WIN_DEV]


VMEM = pl.BlockSpec(memory_space=pltpu.VMEM)
ANY = pl.BlockSpec(memory_space=pl.ANY)


def body(windows, partner_dev, partner_slot):
    side = (2 * WIN, 256)
    dma = pltpu.SemaphoreType.DMA
    rows = pl.pallas_call(
        flow_kernel,
        out_shape=jax.ShapeDtypeStruct((8, 128), F32),
        in_specs=[ANY, VMEM, VMEM] + [ANY] * 6,
        out_specs=VMEM,
        scratch_shapes=[
            pltpu.VMEM((PHASES, 256, 256), BF16),
            pltpu.VMEM((2 * WIN, 2 * WIN), BF16),
            pltpu.VMEM((2 * QROWS, 2 * WIN), BF16),
            pltpu.VMEM((512, 128), BF16),
            pltpu.VMEM((256, 128), BF16),
            pltpu.VMEM((8, 128), BF16),
            pltpu.VMEM((WIN_DEV, WIN * WIN), BF16),
            pltpu.VMEM((WIN * WIN_DEV, 128), F32),
            pltpu.VMEM((WIN * WIN_DEV, 128), F32),
            pltpu.VMEM((WIN_DEV, 2 * WIN, 128), BF16),
            pltpu.VMEM((GROUPS,) + side, BF16),
            pltpu.VMEM((STEPS_DEV,) + side, BF16),
            pltpu.VMEM((BATCH,) + side, BF16),
            pltpu.VMEM((SHARE,) + side, BF16),
            pltpu.VMEM((STEPS_DEV,) + side, BF16),
            pltpu.VMEM((BATCH,) + side, BF16),
            pltpu.VMEM((BATCH * QROWS, 512), BF16),
            pltpu.VMEM((BATCH * 16, 256), F32),
            pltpu.VMEM((128, 128), F32),
            pltpu.VMEM((1, 128), jnp.int32),
            pltpu.VMEM((1, 128), jnp.int32),
            pltpu.VMEM((REGIONS, 128), jnp.int32),
            pltpu.SMEM((REGIONS, 128), jnp.int32),
            pltpu.VMEM((128, CAP * 128), BF16),
            pltpu.VMEM((128, CAP * 128), BF16),
            pltpu.VMEM((128, 128), BF16),
            pltpu.VMEM((2, 8, 128), F32),
            pltpu.VMEM((SECTIONS, 24, 128), F32),
            pltpu.VMEM((EARLY, 8, 128), F32),
            pltpu.VMEM((STEPS_DEV - EARLY, SECTIONS, 8, 128), F32),
            pltpu.VMEM((8, 128), F32),
            pltpu.VMEM((8, 128), F32),
            pltpu.VMEM((REGIONS - 1, 8, 128), F32),
            dma((PARTS + 6,)),
            dma,
            dma((5,)),
            dma((SHARE // CHUNK,)),
            dma((STEPS_DEV,)),
            dma((STEPS_DEV,)),
            dma,
            dma,
            dma,
            dma,
            dma,
            dma,
            dma,
            dma,
            pltpu.SemaphoreType.REGULAR,
        ],
        compiler_params=pltpu.CompilerParams(
            vmem_limit_bytes=60 << 20, collective_id=0, has_side_effects=True
        ),
        name="flows",
    )(windows, partner_dev, partner_slot, *tables())
    out = jax.ShapeDtypeStruct((1, 2, WIN_DEV), F32)
    return pl.pallas_call(
        split_kernel,
        out_shape=(out, out, out),
        in_specs=[VMEM],
        out_specs=(VMEM, VMEM, VMEM),
        name="split",
    )(rows)


def solution(mesh):
    placed = (P("sec", "region", None), P("region"), P("region"))
    return jax.shard_map(
        body,
        mesh=mesh,
        in_specs=placed,
        out_specs=(P("sec", None, "region"),) * 3,
        check_vma=False,
    )
```

```python
import functools
import math

import jax
import jax.numpy as jnp
import ml_dtypes
import numpy as np
from jax import lax
from jax.experimental import pallas as pl
from jax.experimental.pallas import tpu as pltpu
from jax.sharding import PartitionSpec as P

WIN = 160
RADIUS = 16
SHIFTS = 33
ITERS = 32
HALF = WIN // 2 + 1
CAP = 3
REGIONS = 32
SECTIONS = 4
WIN_DEV = 48
GROUPS = WIN_DEV // CAP
SHARE = 12
CHUNK = 4
QROWS = 48
TLANES = 40
PHASES = 4
QUARTER = WIN // PHASES
PARTS = 5
STEPS_DEV = REGIONS // 2
EARLY = STEPS_DEV - 2
BATCH = 6
QUARTERS = GROUPS // CHUNK

sharpness = 12.0
montage_stiffness = 1.0
section_stiffness = 1.0
anchor_stiffness = 0.05
step_length = 0.2

F32 = jnp.float32
BF16 = jnp.bfloat16
MESH = pl.DeviceIdType.MESH
EMPTY = 1 << 20


def tables():
    f32 = np.float32
    index = np.arange(WIN)
    step = f32(2.0 * math.pi / WIN)

    def rounded(fn, phase):
        angle = (phase % WIN).astype(f32) * step
        return fn(angle.astype(np.float64)).astype(f32).astype(ml_dtypes.bfloat16).astype(f32)

    phase = index[:, None] * index[None, :]
    cosine, sine = rounded(np.cos, phase), rounded(np.sin, phase)
    back = (np.arange(SHIFTS) - RADIUS)[:, None] * index[None, :]
    back_cos, back_sin = rounded(np.cos, back), rounded(np.sin, back)

    right = np.zeros((PHASES, 256, 256), f32)
    for m in range(PHASES):
        rows = slice(32 * m, 32 * m + WIN)
        right[m, rows, :HALF] = cosine[:, :HALF]
        right[m, rows, 128 : 128 + HALF] = -sine[:, :HALF]
    order = np.concatenate([np.arange(QUARTER) * PHASES + m for m in range(PHASES)])
    c, s = cosine[:, order], sine[:, order]
    left = np.concatenate([np.concatenate([c, s], 1), np.concatenate([-s, c], 1)], 0)
    back_left = np.zeros((2 * QROWS, 2 * WIN), f32)
    back_left[:SHIFTS] = np.concatenate([back_cos, -back_sin], 1)
    back_left[QROWS : QROWS + SHIFTS] = np.concatenate([back_sin, back_cos], 1)
    weight = np.full(HALF, 2.0, f32)
    weight[0] = weight[-1] = 1.0
    back_right = np.zeros((512, 128), f32)
    energy = np.zeros((256, 128), f32)
    member = np.zeros((8, 128), f32)
    for i in range(CAP):
        rows, lanes = HALF * i, TLANES * i
        back_right[rows : rows + HALF, lanes : lanes + SHIFTS] = weight[:, None] * back_cos[:, :HALF].T
        back_right[256 + rows : 256 + rows + HALF, lanes : lanes + SHIFTS] = (
            -weight[:, None] * back_sin[:, :HALF].T
        )
        energy[rows : rows + HALF, lanes : lanes + TLANES] = weight[:, None]
        member[i::CAP, lanes : lanes + SHIFTS] = 1.0
    member[2 * CAP :] = 0.0
    return [jnp.asarray(t.astype(ml_dtypes.bfloat16)) for t in (right, left, back_left, back_right, energy, member)]


def split3(x):
    high = x.astype(BF16)
    rest = x - high.astype(F32)
    middle = rest.astype(BF16)
    low = (rest - middle.astype(F32)).astype(BF16)
    return high, middle, low


def exact_dot(x, table):
    rows = x.shape[0]
    out = jnp.dot(jnp.concatenate(split3(x), axis=0), table, preferred_element_type=F32)
    return out[:rows] + out[rows : 2 * rows] + out[2 * rows :]


def lane_iota(rows=1):
    return lax.broadcasted_iota(jnp.int32, (rows, 128), 1)


SECTION_RECV = (
    ((1, 0), (1, 1), (1, 2)),
    ((0, 3), (2, 0), (2, 1)),
    ((1, 2), (1, 3), (3, 0)),
    ((2, 1), (2, 2), (2, 3)),
)


STEPS = (
    (0, 0, 2), (1, 0, 2), "y", (0, 0, 1), (2, 0, -1), (1, 0, 0), (-1, 0, 1), (1, 0, 1),
    (1, 1, -1), (2, 1, 1), (-1, 1, -1), "xz", (-1, 1, 0), (0, 1, -1), (-1, 1, 2), "x",
)
MUTUAL = STEPS.index((0, 0, 2))


def moved(me, step, sign):
    y, x, z = me // 8, me // 4 % 2, me % 4
    move = STEPS[step]
    if move == "y":
        upper = y // 2
        move = (2, 0, 2 * (1 - upper) if sign > 0 else 2 * upper)
    elif isinstance(move, str):
        move = (2 * (1 - x) if sign > 0 else 2 * x, 1, 2 if move == "xz" else 0)
    dy, dx, dz = move
    return (y + sign * dy + 4) % 4 * 8 + (x + dx) % 2 * 4 + (z + sign * dz + 4) % 4


def section_sends(section):
    return [
        (to, source, chunk)
        for to in range(SECTIONS)
        for chunk, (origin, source) in enumerate(SECTION_RECV[to])
        if origin == section
    ]


def flow_kernel(
    win_hbm, dev_ref, slot_ref,
    right_hbm, left_hbm, back_left_hbm, back_right_hbm, energy_hbm, member_hbm,
    out_ref,
    right_ref, left_ref, back_left_ref, back_right_ref, energy_ref, member_ref,
    win_ref, seg_re, seg_im, spectra, natural, outgoing, packed, from_section, from_region,
    cross, backs, squares, sums, dev_row, slot_row, ids_vmem, ids,
    from_slot, from_group, from_partner, published, ours, early, late, sections, field, fields,
    load_sem, ids_sem, sec_send, sec_recv, reg_send, reg_recv,
    field_send, field_recv, ours_send, ours_recv, early_send, early_recv, late_send, late_recv, ready,
):
    me = lax.axis_index("region")
    sec = lax.axis_index("sec")

    def neighbour(o):
        return {"region": (me + o) % REGIONS}

    width = WIN * WIN // PARTS
    load_right = pltpu.make_async_copy(right_hbm, right_ref, load_sem.at[PARTS])
    load_tables = [
        pltpu.make_async_copy(source, into, load_sem.at[PARTS + 1 + k])
        for k, (source, into) in enumerate(
            (
                (left_hbm, left_ref),
                (back_left_hbm, back_left_ref),
                (back_right_hbm, back_right_ref),
                (energy_hbm, energy_ref),
                (member_hbm, member_ref),
            )
        )
    ]

    def load_part(part):
        lanes = pl.ds(part * width, width)
        return pltpu.make_async_copy(
            win_hbm.at[0, :, lanes], win_ref.at[:, lanes], load_sem.at[part]
        )

    load_right.start()
    for part in range(PARTS):
        load_part(part).start()

    barrier = pltpu.get_barrier_semaphore()

    def greet(o, _):
        pl.semaphore_signal(barrier, inc=1, device_id=neighbour(o), device_id_type=MESH)
        return 0

    lax.fori_loop(1, REGIONS, greet, 0)
    for d in range(1, SECTIONS):
        pl.semaphore_signal(
            barrier, inc=1, device_id={"sec": (sec + d) % SECTIONS}, device_id_type=MESH
        )
    for load in load_tables:
        load.start()

    load_right.wait()
    for part in range(PARTS):
        load_part(part).wait()
        for m in range(PHASES):
            rows = [
                win_ref[:, 640 * q + 128 * m : 640 * q + 128 * m + 256]
                for q in range(8 * part, 8 * part + 8)
            ]
            seg = jnp.dot(
                jnp.concatenate(rows, axis=0), right_ref[m], preferred_element_type=F32
            )
            start = (QUARTER * m + 8 * part) * WIN_DEV
            seg_re[start : start + 8 * WIN_DEV, :] = seg[:, :128]
            seg_im[start : start + 8 * WIN_DEV, :] = seg[:, 128:]
    for load in load_tables:
        load.wait()

    wide = lane_iota(2 * WIN)

    def pack(windows):
        x0, x1, x2 = [spectra[w] for w in windows]
        x1 = pltpu.roll(x1, HALF, 1)
        x2 = pltpu.roll(x2, 2 * HALF - 128, 1)
        return jnp.concatenate(
            [jnp.where(wide < HALF, x0, x1), jnp.where(wide < 2 * HALF - 128, x1, x2)], axis=1
        )

    def section_copy(k, index):
        to, source, chunk = section_sends(k)[index]
        return pltpu.make_async_remote_copy(
            src_ref=natural.at[pl.ds(CHUNK * source, CHUNK)],
            dst_ref=from_section.at[pl.ds(CHUNK * chunk, CHUNK)],
            send_sem=sec_send.at[index],
            recv_sem=sec_recv.at[chunk],
            device_id={"sec": to},
            device_id_type=MESH,
        )

    def region_copy(step):
        to = moved(me, step, 1)
        return pltpu.make_async_remote_copy(
            src_ref=outgoing.at[step],
            dst_ref=from_region.at[step],
            send_sem=reg_send.at[step],
            recv_sem=reg_recv.at[step],
            device_id={"region": to},
            device_id_type=MESH,
        )

    def spectra_step(step, first):
        part = (2 * first + step) % (2 * QUARTERS)
        for pair in range(CAP):
            w = 2 * CAP * part + 2 * pair
            sides = [
                jnp.concatenate(
                    [seg[pl.ds(w + k, WIN, stride=WIN_DEV), :] for k in range(2)], axis=1
                ).astype(BF16)
                for seg in (seg_re, seg_im)
            ]
            spectrum = jnp.dot(
                left_ref[...], jnp.concatenate(sides, axis=0), preferred_element_type=F32
            ).astype(BF16)
            spectra[w] = spectrum[:, :128]
            spectra[w + 1] = spectrum[:, 128:]
        for k in range(2):
            w = 2 * CAP * part + CAP * k
            natural[2 * part + k] = pack([w, w + 1, w + 2])
        return first

    lane = lane_iota()
    start = jnp.where(sec == 1, 2, 0)
    for quarter in range(QUARTERS):
        lax.fori_loop(2 * quarter, 2 * quarter + 2, spectra_step, start, unroll=True)
        if quarter == 0:
            pl.semaphore_wait(barrier, REGIONS - 1 + SECTIONS - 1)
            for d in range(1, SECTIONS):
                pl.semaphore_signal(
                    ready, inc=1, device_id={"sec": (sec + d) % SECTIONS}, device_id_type=MESH
                )
        for k in range(SECTIONS):
            done = (quarter + (2 if k == 1 else 0)) % QUARTERS

            @pl.when(sec == k)
            def _():
                for index, (_, source, _) in enumerate(section_sends(k)):
                    if source == done:
                        section_copy(k, index).start()

        if quarter != 1:
            continue
        dev_row[...] = jnp.full((1, 128), -1, jnp.int32)
        slot_row[...] = jnp.full((1, 128), -1, jnp.int32)
        dev_row[0:1, 0:WIN_DEV] = dev_ref[...].reshape(1, WIN_DEV)
        slot_row[0:1, 0:WIN_DEV] = slot_ref[...].reshape(1, WIN_DEV)
        device, partner = dev_row[...], slot_row[...]
        code = jnp.where(me < device, lane, partner) * 64 + lane
        same = device == lax.broadcasted_iota(jnp.int32, (REGIONS, 128), 0)
        left_over = jnp.where(same, code, EMPTY)
        rank = jnp.zeros((1, 128), jnp.int32)
        listed = jnp.zeros((REGIONS, 128), jnp.int32)
        lane32 = lane_iota(REGIONS)
        for i in range(CAP):
            least = jnp.min(left_over, axis=1, keepdims=True)
            found = jnp.logical_and(same, left_over == least)
            rank += i * jnp.sum(jnp.where(found, 1, 0), axis=0, keepdims=True)
            window = jnp.where(least < EMPTY, least % 64, 0)
            listed = jnp.where(lane32 == i, window, listed)
            left_over = jnp.where(left_over > least, left_over, EMPTY)
        ids_vmem[...] = listed
        load_ids = pltpu.make_async_copy(ids_vmem, ids, ids_sem)
        load_ids.start()

    load_ids.wait()

    across = STEPS_DEV // 2
    for step in [n + k for n in range(across) for k in (across, 0)]:
        to = moved(me, step, 1)
        outgoing[step] = pack([ids[to, i] for i in range(CAP)])
        region_copy(step).start()

    row = lax.broadcasted_iota(jnp.int32, (128, 128), 0)
    column = lax.broadcasted_iota(jnp.int32, (128, 128), 1)
    origin = jnp.full((128, 128), -2, jnp.int32)
    for step in range(STEPS_DEV):
        origin = jnp.where(row == step, moved(me, step, -1), origin)
        if step != MUTUAL:
            origin = jnp.where(row == STEPS_DEV + step, moved(me, step, 1), origin)
    sign = jnp.where(row < STEPS_DEV, 1.0, -1.0)
    for i in range(CAP):
        chosen = jnp.logical_and(origin == device, rank == i)
        from_slot[:, 128 * i : 128 * i + 128] = jnp.where(chosen, sign, 0.0).astype(BF16)
        chosen = CAP * row + i == column
        chosen = jnp.logical_and(chosen, column < WIN_DEV)
        from_group[:, 128 * i : 128 * i + 128] = chosen.astype(F32).astype(BF16)
    from_partner[...] = (row == partner).astype(F32).astype(BF16)

    sums[...] = jnp.zeros_like(sums)
    row_shift = lax.broadcasted_iota(jnp.int32, (QROWS, 128), 0)
    shift_mask = jnp.logical_and(row_shift < SHIFTS, lane_iota(QROWS) % TLANES < SHIFTS)
    row_value = (row_shift - RADIUS).astype(F32)

    def correlate(first_ref, second_ref, u):
        energy_a = jnp.zeros((8, 256), F32)
        energy_b = jnp.zeros((8, 256), F32)
        for r in range(0, WIN, 32):
            ar = first_ref[r : r + 32, :].astype(F32)
            ai = first_ref[WIN + r : WIN + r + 32, :].astype(F32)
            br = second_ref[r : r + 32, :].astype(F32)
            bi = second_ref[WIN + r : WIN + r + 32, :].astype(F32)
            scale = 1.0 / (WIN * WIN)
            cross[u, r : r + 32, :] = ((ar * br + ai * bi) * scale).astype(BF16)
            cross[u, WIN + r : WIN + r + 32, :] = ((ai * br - ar * bi) * scale).astype(BF16)
            energy_a += jnp.sum((ar * ar + ai * ai).reshape(4, 8, 256), axis=0)
            energy_b += jnp.sum((br * br + bi * bi).reshape(4, 8, 256), axis=0)
        squares[16 * u : 16 * u + 8, :] = energy_a
        squares[16 * u + 8 : 16 * u + 16, :] = energy_b
        back = jnp.dot(back_left_ref[...], cross[u], preferred_element_type=F32).astype(BF16)
        backs[QROWS * u : QROWS * u + QROWS, :256] = back[:QROWS]
        backs[QROWS * u : QROWS * u + QROWS, 256:] = back[QROWS:]

    column_value = (lane % TLANES - RADIUS).astype(F32)
    lane8 = lane_iota(8)
    row8 = lax.broadcasted_iota(jnp.int32, (8, 128), 0)

    def weigh(count):
        surfaces = jnp.dot(
            backs[: QROWS * count], back_right_ref[...], preferred_element_type=F32
        )
        energies = exact_dot(squares[: 16 * count], energy_ref[...]) / (WIN * WIN)
        for u in range(count):
            first = jnp.sum(energies[16 * u : 16 * u + 8], axis=0, keepdims=True)
            second = jnp.sum(energies[16 * u + 8 : 16 * u + 16], axis=0, keepdims=True)
            norm = jnp.sqrt(first * second + 1e-06)
            surface = surfaces[QROWS * u : QROWS * u + QROWS]
            weights = jnp.where(shift_mask, jnp.exp(sharpness * (surface / norm)), 0.0)
            total = jnp.sum(weights, axis=0, keepdims=True)
            sums[u : u + 1, :] = total
            sums[8 + u : 9 + u, :] = jnp.sum(weights * row_value, axis=0, keepdims=True)
            sums[16 + u : 17 + u, :] = total * column_value
        parts = [
            lax.dot_general(
                member_ref[...], part, (((1,), (1,)), ((), ())), preferred_element_type=F32
            )
            for part in split3(sums[...])
        ]
        total = parts[0] + parts[1] + parts[2]
        moment = jnp.where(row8 < CAP, pltpu.roll(total, 128 - 8, 1), pltpu.roll(total, 128 - 16, 1))
        flows = moment / jnp.where(total == 0.0, 1.0, total)
        return jnp.where(jnp.logical_and(jnp.abs(flows) <= 2.0 * RADIUS, lane8 < count), flows, 0.0)

    def section_batch(chunk, _):
        pltpu.make_async_remote_copy(
            src_ref=natural.at[pl.ds(0, CHUNK)],
            dst_ref=from_section.at[pl.ds(CHUNK * chunk, CHUNK)],
            send_sem=sec_send.at[0],
            recv_sem=sec_recv.at[chunk],
            device_id={"sec": (sec + 1) % SECTIONS},
            device_id_type=MESH,
        ).wait_recv()
        first = CHUNK * ((SHARE // CHUNK * sec + chunk) % QUARTERS)
        for u in range(CHUNK):
            correlate(natural.at[first + u], from_section.at[CHUNK * chunk + u], u)
        flows = weigh(CHUNK)
        flows = jnp.where(chunk < sec, -flows, flows)
        sections[...] += pltpu.roll(flows, CHUNK * chunk, 1)
        return 0

    def early_copy(step):
        return pltpu.make_async_remote_copy(
            src_ref=published.at[0],
            dst_ref=early.at[step],
            send_sem=early_send,
            recv_sem=early_recv,
            device_id={"region": moved(me, step, -1)},
            device_id_type=MESH,
        )

    def late_copy(step, k):
        return pltpu.make_async_remote_copy(
            src_ref=published.at[1],
            dst_ref=late.at[step - EARLY, sec],
            send_sem=late_send,
            recv_sem=late_recv,
            device_id={"sec": k, "region": moved(me, step, -1)},
            device_id_type=MESH,
        )

    def ours_copy(d):
        return pltpu.make_async_remote_copy(
            src_ref=ours.at[0],
            dst_ref=ours.at[d],
            send_sem=ours_send,
            recv_sem=ours_recv,
            device_id={"sec": (sec + d) % SECTIONS},
            device_id_type=MESH,
        )

    def field_copy(o):
        return pltpu.make_async_remote_copy(
            src_ref=field,
            dst_ref=fields.at[REGIONS - 1 - o],
            send_sem=field_send,
            recv_sem=field_recv,
            device_id=neighbour(o),
            device_id_type=MESH,
        )

    def region_batch(first, last):
        for u, step in enumerate(range(first, last)):
            origin = moved(me, step, -1)
            packed[u] = pack([ids[origin, i] for i in range(CAP)])
            region_copy(step).wait_recv()
            correlate(packed.at[u], from_region.at[step], u)
        flows = weigh(last - first)
        flows += pltpu.roll(flows, STEPS_DEV, 1)
        return pltpu.roll(flows, first, 1) if first else flows

    def by_window(x, table):
        spread = exact_dot(x, table)
        rows = []
        for k in range(x.shape[0] // 8):
            for c in range(2):
                at = 8 * k + CAP * c
                rows.append(
                    sum(spread[at + i : at + i + 1, 128 * i : 128 * i + 128] for i in range(CAP))
                )
        return rows

    sections[...] = jnp.zeros((8, 128), F32)
    chunks = SHARE // CHUNK
    low = jnp.where(sec == 2, chunks - 1, 0)
    high = jnp.where(sec == 1, 1, chunks)
    lax.fori_loop(low, high, section_batch, 0)
    flows = region_batch(0, 4)
    lax.fori_loop(0, low, section_batch, 0)
    lax.fori_loop(high, chunks, section_batch, 0)
    section = sections[...]
    shift = section
    for k in range(1, SECTIONS):
        shift = jnp.where(sec == k, pltpu.roll(section, SHARE * k, 1), shift)
    edges = [shift] + [pltpu.roll(shift, 128 - GROUPS * e, 1) for e in range(1, SECTIONS - 1)]
    edges = [jnp.where(lane8 < GROUPS, edge, 0.0) for edge in edges]
    section_rows = by_window(jnp.concatenate(edges, axis=0), from_group[...])
    section = jnp.concatenate(section_rows + [jnp.zeros((2, 128), F32)], axis=0)
    field[...] = section

    def field_start(o, _):
        field_copy(o).start()
        return 0

    lax.fori_loop(1, REGIONS, field_start, 0)
    pl.semaphore_wait(ready, SECTIONS - 1)
    flows += region_batch(4, 8)
    flows += region_batch(8, EARLY)
    published[0] = flows
    for step in range(EARLY):
        early_copy(step).start()
    flows += region_batch(EARLY, STEPS_DEV)
    published[1] = flows
    for step in range(EARLY, STEPS_DEV):
        for k in range(SECTIONS):
            late_copy(step, k).start()

    pltpu.make_async_copy(fields, fields, field_recv).wait()
    found = exact_dot(fields[...].reshape(8 * (REGIONS - 1), 128), from_partner[...])
    partner_section = jnp.zeros((8, 128), F32)
    for o in range(1, REGIONS):
        here = jnp.broadcast_to(device, (8, 128)) == (me + o) % REGIONS
        partner_section = jnp.where(here, found[8 * o - 8 : 8 * o], partner_section)
    pltpu.make_async_copy(early, early, early_recv).wait()
    for step in range(EARLY):
        flows = jnp.where(lane8 == STEPS_DEV + step, early[step], flows)
    ours[0, 0:8, :] = flows
    ours[0, 8:16, :] = section
    ours[0, 16:24, :] = partner_section
    for d in range(1, SECTIONS):
        ours_copy(d).start()
    for k in range(SECTIONS):

        @pl.when(sec == k)
        def _():
            for index in range(len(section_sends(k))):
                section_copy(k, index).wait_send()

    for step in range(STEPS_DEV):
        region_copy(step).wait_send()
    pltpu.make_async_copy(fields, fields, field_send).wait()
    pltpu.make_async_copy(early, early, early_send).wait()
    pltpu.make_async_copy(late, late, late_recv).wait()
    others = ours.at[pl.ds(1, SECTIONS - 1)]
    pltpu.make_async_copy(others, others, ours_recv).wait()
    blocks = []
    for k in range(SECTIONS):
        block = ours[(sec - k + SECTIONS) % SECTIONS, 0:8, :]
        for step in range(EARLY, STEPS_DEV):
            block = jnp.where(lane8 == STEPS_DEV + step, late[step - EARLY, k], block)
        blocks.append(block)
    montage = jnp.concatenate(
        by_window(jnp.concatenate(blocks, axis=0), from_slot[...]), axis=0
    )
    section = ours[0, 8:16, :] + ours[1, 8:16, :] + ours[2, 8:16, :] + ours[3, 8:16, :]
    partner_section = ours[0, 16:24, :] + ours[1, 16:24, :] + ours[2, 16:24, :] + ours[3, 16:24, :]

    has_next = jnp.where(row8 < 2 * (SECTIONS - 1), 1.0, 0.0)
    has_prev = jnp.where(row8 >= 2, 1.0, 0.0)
    disagreement = 2.0 * montage

    def before(x):
        return pltpu.roll(x, 2, 0)

    def after(x):
        return pltpu.roll(x, 6, 0)

    def relax(u, p, apart, flow, previous):
        gradient = (
            montage_stiffness * (2.0 * u - 2.0 * p - apart)
            + section_stiffness * has_next * (u - after(u) - flow)
            - section_stiffness * has_prev * (before(u) - u - previous)
            + anchor_stiffness * u
        )
        return u - step_length * gradient

    previous, partner_previous = before(section), before(partner_section)

    def turn(_, state):
        u, p = state
        return (
            relax(u, p, disagreement, section, previous),
            relax(p, u, -disagreement, partner_section, partner_previous),
        )

    zero = jnp.zeros((8, 128), F32)
    shift, _ = lax.fori_loop(0, ITERS, turn, (zero, zero))
    for k, values in enumerate((montage, section, shift)):
        chosen = values[0:2]
        for n in range(1, SECTIONS):
            chosen = jnp.where(sec == n, values[2 * n : 2 * n + 2], chosen)
        out_ref[2 * k : 2 * k + 2, :] = chosen
    out_ref[6:8, :] = jnp.zeros((2, 128), F32)

    pltpu.make_async_copy(late, late, late_send).wait()
    pltpu.make_async_copy(others, others, ours_send).wait()


def split_kernel(rows_ref, montage_ref, section_ref, shift_ref):
    for k, ref in enumerate((montage_ref, section_ref, shift_ref)):
        ref[0] = rows_ref[2 * k : 2 * k + 2, :WIN_DEV]


VMEM = pl.BlockSpec(memory_space=pltpu.VMEM)
ANY = pl.BlockSpec(memory_space=pl.ANY)


def body(windows, partner_dev, partner_slot):
    side = (2 * WIN, 256)
    dma = pltpu.SemaphoreType.DMA
    rows = pl.pallas_call(
        flow_kernel,
        out_shape=jax.ShapeDtypeStruct((8, 128), F32),
        in_specs=[ANY, VMEM, VMEM] + [ANY] * 6,
        out_specs=VMEM,
        scratch_shapes=[
            pltpu.VMEM((PHASES, 256, 256), BF16),
            pltpu.VMEM((2 * WIN, 2 * WIN), BF16),
            pltpu.VMEM((2 * QROWS, 2 * WIN), BF16),
            pltpu.VMEM((512, 128), BF16),
            pltpu.VMEM((256, 128), BF16),
            pltpu.VMEM((8, 128), BF16),
            pltpu.VMEM((WIN_DEV, WIN * WIN), BF16),
            pltpu.VMEM((WIN * WIN_DEV, 128), F32),
            pltpu.VMEM((WIN * WIN_DEV, 128), F32),
            pltpu.VMEM((WIN_DEV, 2 * WIN, 128), BF16),
            pltpu.VMEM((GROUPS,) + side, BF16),
            pltpu.VMEM((STEPS_DEV,) + side, BF16),
            pltpu.VMEM((BATCH,) + side, BF16),
            pltpu.VMEM((SHARE,) + side, BF16),
            pltpu.VMEM((STEPS_DEV,) + side, BF16),
            pltpu.VMEM((BATCH,) + side, BF16),
            pltpu.VMEM((BATCH * QROWS, 512), BF16),
            pltpu.VMEM((BATCH * 16, 256), F32),
            pltpu.VMEM((128, 128), F32),
            pltpu.VMEM((1, 128), jnp.int32),
            pltpu.VMEM((1, 128), jnp.int32),
            pltpu.VMEM((REGIONS, 128), jnp.int32),
            pltpu.SMEM((REGIONS, 128), jnp.int32),
            pltpu.VMEM((128, CAP * 128), BF16),
            pltpu.VMEM((128, CAP * 128), BF16),
            pltpu.VMEM((128, 128), BF16),
            pltpu.VMEM((2, 8, 128), F32),
            pltpu.VMEM((SECTIONS, 24, 128), F32),
            pltpu.VMEM((EARLY, 8, 128), F32),
            pltpu.VMEM((STEPS_DEV - EARLY, SECTIONS, 8, 128), F32),
            pltpu.VMEM((8, 128), F32),
            pltpu.VMEM((8, 128), F32),
            pltpu.VMEM((REGIONS - 1, 8, 128), F32),
            dma((PARTS + 6,)),
            dma,
            dma((5,)),
            dma((SHARE // CHUNK,)),
            dma((STEPS_DEV,)),
            dma((STEPS_DEV,)),
            dma,
            dma,
            dma,
            dma,
            dma,
            dma,
            dma,
            dma,
            pltpu.SemaphoreType.REGULAR,
        ],
        compiler_params=pltpu.CompilerParams(
            vmem_limit_bytes=60 << 20, collective_id=0, has_side_effects=True
        ),
        name="flows",
    )(windows, partner_dev, partner_slot, *tables())
    out = jax.ShapeDtypeStruct((1, 2, WIN_DEV), F32)
    return pl.pallas_call(
        split_kernel,
        out_shape=(out, out, out),
        in_specs=[VMEM],
        out_specs=(VMEM, VMEM, VMEM),
        name="split",
    )(rows)


def solution(mesh):
    placed = (P("sec", "region", None), P("region"), P("region"))
    return jax.shard_map(
        body,
        mesh=mesh,
        in_specs=placed,
        out_specs=(P("sec", None, "region"),) * 3,
        check_vma=False,
    )
```
